512 devices in a mesh: trc: 8 (over y_lo, core), ty: 4 (over x), tx: 16 (over z, y_hi).
Axes of the slice: x: 4, y: 8 (y_hi: 2, y_lo: 4; y = y_hi * 4 + y_lo), z: 8, core: 2. Of those that a mesh axis runs over, the one named last changes fastest.
Arguments:
- tracers: float32 [80, 8, 64, 2048], P('trc', None, 'ty', 'tx'), may hold values from -6 to 6
- courant: float32 [2, 8, 64, 2048], P(None, 'trc', 'ty', 'tx'), may hold values from -0.9 to 0.9
- assignment: int32 [80], replicated, may hold values from 0 to 79, each once
- species_gain: float32 [80], replicated, may hold values from 0.3 to 3
- w_in: bfloat16 [256, 80], replicated, may hold values from -0.625 to 0.625
- b_in: float32 [256], replicated, may hold values from -3 to 3
- w_mid: bfloat16 [2, 256, 256], replicated, may hold values from -0.375 to 0.375
- b_mid: float32 [2, 256], replicated, may hold values from -3 to 3
- w_out: bfloat16 [80, 256], replicated, may hold values from -0.375 to 0.375
- b_out: float32 [80], replicated, may hold values from -3 to 3
Outputs:
- updated: float32 [80, 8, 64, 2048], P('trc', None, 'ty', 'tx')
The draws below stay inside these ranges and needn't reach their ends.
Inputs may be any that keep to these rules, and one draw needn't show every extreme that they name: `assignment`: each species stands in exactly one tracer slot.
All inputs are finite; a program needn't handle non-finite values.
Results may differ from the reference program's by a relative error of at most 0.0029.
Values sent between devices are 32-bit elements; how exact they have to be, the bound alone decides.
A program may use at most 64 MiB of HBM per device.

```python
import math
import jax
import jax.numpy as jnp
from jax import lax

NSPEC = 80
HID = 256
MIDL = 2
LEV = 8
NSUB = 1
NY = 64
NX = 2048


def level_of(rng, dims, split, least, high):
    factor_of = 1.0
    for axis_at, parts in split:
        heights = jax.random.uniform(jax.random.fold_in(jax.random.fold_in(rng, 6), axis_at), (parts,), jnp.float32, least / len(split), high / len(split))
        factor_of = factor_of * jnp.repeat(jnp.exp(heights), dims[axis_at] // parts).reshape((-1,) + (1,) * (len(dims) - 1 - axis_at))
    return factor_of


def centred(stream_key, shape, scale, reach, cuts=(), kind=jnp.bfloat16):
    values = jax.random.normal(stream_key, shape, jnp.float32) * scale
    if len(cuts) > 0:
        values = level_of(stream_key, shape, cuts, -0.22, 0.18) * values
    return jnp.clip(values, min=-reach, max=reach).astype(kind)


def setup_inputs(seed: int = 0) -> dict:
    splits = jax.random.split(jax.random.key(seed), 11)
    return {
        "tracers": centred(splits[0], (NSPEC, LEV, NY, NX), 1.0, 6.0, ((0, 8), (2, 4), (3, 16)), jnp.float32),
        "courant": jnp.clip(jax.random.uniform(splits[1], (2, LEV, NY, NX), jnp.float32, -0.9, 0.9) * level_of(splits[1], (2, LEV, NY, NX), ((1, 8), (2, 4), (3, 16)), -0.4, 0.0), -0.9, 0.9),
        "assignment": jax.random.permutation(splits[2], NSPEC).astype(jnp.int32),
        "species_gain": jnp.clip(jnp.exp(jax.random.uniform(splits[3], (NSPEC,), jnp.float32, math.log(0.3), math.log(3.0))), 0.3, 3.0),
        "w_in": centred(splits[4], (HID, NSPEC), NSPEC ** -0.5, 0.625),
        "b_in": centred(splits[5], (HID,), 0.5, 3.0, (), jnp.float32),
        "w_mid": centred(splits[6], (MIDL, HID, HID), HID ** -0.5, 0.375),
        "b_mid": centred(splits[7], (MIDL, HID), 0.5, 3.0, (), jnp.float32),
        "w_out": centred(splits[8], (NSPEC, HID), HID ** -0.5, 0.375),
        "b_out": centred(splits[9], (NSPEC,), 0.5, 3.0, (), jnp.float32),
    }


def cut_range(values, begin_at, end_at, along):
    return lax.slice_in_dim(values, begin_at, end_at, axis=along)


def parabolic_sweep(padded, speeds, along):
    count = padded.shape[along] - 6
    edge_values = (7.0 / 12.0) * (cut_range(padded, 1, count + 4, along) + cut_range(padded, 2, count + 5, along)) - (1.0 / 12.0) * (cut_range(padded, 0, count + 3, along) + cut_range(padded, 3, count + 6, along))
    left_edge = cut_range(edge_values, 0, count + 2, along)
    right_edge = cut_range(edge_values, 1, count + 3, along)
    centre = cut_range(padded, 2, count + 4, along)
    edge_slope = right_edge - left_edge
    curvature = 6.0 * (centre - 0.5 * (left_edge + right_edge))
    face_speed = 0.5 * (cut_range(speeds, 2, count + 3, along) + cut_range(speeds, 3, count + 4, along))
    from_left = face_speed * (cut_range(right_edge, 0, count + 1, along) - 0.5 * face_speed * (cut_range(edge_slope, 0, count + 1, along) - (1.0 - face_speed * (2.0 / 3.0)) * cut_range(curvature, 0, count + 1, along)))
    from_right = face_speed * (cut_range(left_edge, 1, count + 2, along) - 0.5 * face_speed * (cut_range(edge_slope, 1, count + 2, along) + (1.0 + face_speed * (2.0 / 3.0)) * cut_range(curvature, 1, count + 2, along)))
    face_flux = jnp.where(face_speed > 0.0, from_left, from_right)
    return cut_range(padded, 3, count + 3, along) - (cut_range(face_flux, 1, count + 1, along) - cut_range(face_flux, 0, count, along))


def transport(tracer_field, courant):
    speed_x = jnp.pad(courant[0], ((0, 0), (0, 0), (3, 3)), mode="wrap")
    speed_y = jnp.pad(courant[1], ((0, 0), (3, 3), (0, 0)))
    for substep in range(NSUB):
        tracer_field = parabolic_sweep(jnp.pad(tracer_field, ((0, 0), (0, 0), (3, 3)), mode="wrap"), speed_x, 2)
        tracer_field = parabolic_sweep(jnp.pad(tracer_field, ((0, 0), (3, 3), (0, 0))), speed_y, 1)
    return tracer_field


def reference(tracers, courant, assignment, species_gain, w_in, b_in, w_mid, b_mid, w_out, b_out):
    advected = lax.map(lambda tracer_field: transport(tracer_field, courant), tracers)
    gain_slot = jnp.take(species_gain, assignment)
    w_first = jnp.take(w_in, assignment, axis=1)
    w_last = jnp.take(w_out, assignment, axis=0)
    b_last = jnp.take(b_out, assignment)

    def chemistry(level_block):
        scaled = (level_block * gain_slot[:, None]).astype(jnp.bfloat16)
        hidden = jax.nn.gelu(jnp.dot(w_first, scaled, preferred_element_type=jnp.float32) + b_in[:, None]).astype(jnp.bfloat16)
        for mid_layer in range(MIDL):
            hidden = jax.nn.gelu(jnp.dot(w_mid[mid_layer], hidden, preferred_element_type=jnp.float32) + b_mid[mid_layer][:, None]).astype(jnp.bfloat16)
        tendency = jnp.dot(w_last, hidden, preferred_element_type=jnp.float32) + b_last[:, None]
        return level_block + tendency

    by_level = jnp.transpose(advected, (1, 0, 2, 3)).reshape(LEV, NSPEC, NY * NX)
    result = lax.map(chemistry, by_level).reshape(LEV, NSPEC, NY, NX)
    return jnp.transpose(result, (1, 0, 2, 3))
```

```python
import functools

import jax
import jax.numpy as jnp
from jax import lax
from jax.experimental import pallas as pl
from jax.experimental.pallas import tpu as pltpu
from jax.sharding import PartitionSpec as P

MESH = pl.DeviceIdType.MESH
GROUPS = (5, 4, 4, 3)
STARTS_EVEN = (11, 7, 3, 0)
STARTS_ODD = (0, 5, 9, 13)


def upwind(f):
    up, down = jnp.maximum(f, 0.0), jnp.minimum(f, 0.0)
    p2, m2 = 0.5 * up * up, 0.5 * down * down
    return up, p2, p2 * (1.0 - (2.0 / 3.0) * up), down, m2, m2 * (1.0 + (2.0 / 3.0) * down)


def edge(a, b, c, d):
    return (7.0 / 12.0) * (b + c) - (1.0 / 12.0) * (a + d)


def sweep_lanes(q, coef):
    p1, p2, p3, m1, m2, m3 = coef
    left = edge(pltpu.roll(q, 2, 1), pltpu.roll(q, 1, 1), q, pltpu.roll(q, 127, 1))
    right = pltpu.roll(left, 127, 1)
    slope = right - left
    curve = 6.0 * q - 3.0 * (left + right)
    out_right = p1 * right - p2 * slope + p3 * curve
    out_left = m1 * left - m2 * slope - m3 * curve
    return q - out_right + out_left + pltpu.roll(out_right, 1, 1) - pltpu.roll(out_left, 127, 1)


def gelu(v):
    inner = v * (0.7978845608028654 + (0.7978845608028654 * 0.044715) * (v * v))
    half = 0.5 * v
    return (half + half * jnp.tanh(inner)).astype(jnp.bfloat16)


def column_of(row, size):
    at = lax.broadcasted_iota(jnp.int32, (size, size), 0)
    to = lax.broadcasted_iota(jnp.int32, (size, size), 1)
    return jnp.sum(jnp.where(at == to, row, 0.0), axis=1, keepdims=True)


def kernel(
    x_ref, c_ref, as_ref, gain_ref, win_ref, bin_ref, wmid_ref, bmid_ref, wout_ref, bout_ref,
    o_ref,
    got, swept, strip, fixed, adv, back, cv, c1h, eco, ecl, ecr, t_out, t_in, cc, cf, sc,
    v_as, v_gain, v_win, v_bin, v_wmid, v_bmid, v_wout, v_bout,
    first_w, last_w, bias_b, last_b, gain_b,
    fs, fr, fl, lw, ts, tr, es, er, c1s, c1r, hs, hr, os_, or_, ol,
):
    me, y, x = lax.axis_index("trc"), lax.axis_index("ty"), lax.axis_index("tx")
    even = 1 - lax.rem(y, 2)
    left, right = {"tx": lax.rem(x + 15, 16)}, {"tx": lax.rem(x + 1, 16)}

    def remote(src, dst, send, recv, to):
        return pltpu.make_async_remote_copy(src, dst, send, recv, device_id=to, device_id_type=MESH)

    def peer(d):
        return lax.rem(me + d, 8)

    loads = [
        pltpu.make_async_copy(src, dst, lw.at[i])
        for i, (src, dst) in enumerate((
            (c_ref.at[:, 0], cv), (as_ref, v_as), (gain_ref, v_gain), (win_ref, v_win), (bin_ref, v_bin),
            (wmid_ref, v_wmid), (bmid_ref, v_bmid), (wout_ref, v_wout), (bout_ref, v_bout),
        ))
    ]
    for load in loads:
        load.start()

    c1h[...] = jnp.zeros((2, 8, 128), jnp.float32)
    barrier = pltpu.get_barrier_semaphore()
    for d in range(1, 8):
        pl.semaphore_signal(barrier, inc=1, device_id={"trc": peer(d)}, device_id_type=MESH)
    for to in (left, right, {"ty": lax.rem(y + 3, 4)}, {"ty": lax.rem(y + 1, 4)}):
        pl.semaphore_signal(barrier, inc=1, device_id=to, device_id_type=MESH)

    lane8 = lax.broadcasted_iota(jnp.int32, (8, 128), 1)
    lane16 = lax.broadcasted_iota(jnp.int32, (16, 128), 1)
    row16 = lax.broadcasted_iota(jnp.int32, (16, 128), 0)

    loads[0].wait()
    c0 = cv[0]
    wind = jnp.zeros((16, 128), jnp.float32)
    for i in range(8):
        wind = jnp.where((lane16 // 16 == i) & (row16 % 8 == i), pltpu.roll(c0, (16 * i + 8) % 128, 1), wind)
    eco[...] = jnp.zeros((8, 128), jnp.float32)
    eco[0:1, :] = jnp.sum(wind[0:8], axis=0, keepdims=True)
    eco[1:2, :] = jnp.sum(wind[8:16], axis=0, keepdims=True)

    @pl.when(y == 0)
    def _():
        swept[0:3] = jnp.zeros((3, 80, 128), jnp.float32)

    @pl.when(y == 3)
    def _():
        swept[19:22] = jnp.zeros((3, 80, 128), jnp.float32)

    pl.semaphore_wait(barrier, 11)

    ec_copies = (remote(eco, ecr, es.at[0], er.at[0], left), remote(eco, ecl, es.at[1], er.at[1], right))
    for copy in ec_copies:
        copy.start()
    wind_up = remote(cv.at[1, pl.ds(0, 1)], c1h.at[1, pl.ds(0, 1)], c1s.at[0], c1r.at[0], {"ty": y - 1})
    wind_down = remote(cv.at[1, pl.ds(15, 1)], c1h.at[0, pl.ds(0, 1)], c1s.at[1], c1r.at[1], {"ty": y + 1})

    @pl.when(y > 0)
    def _():
        wind_up.start()

    @pl.when(y < 3)
    def _():
        wind_down.start()

    halves = (8 * even, 8 * (1 - even))

    def forward(p, d):
        k = peer(d)
        rows = pl.ds(pl.multiple_of(halves[p], 8), 8)
        return remote(
            x_ref.at[:, k, rows], got.at[p, pl.ds(10 * me, 10)], fs.at[p, k], fr.at[p, me], {"trc": k}
        )

    def arriving(p, d):
        k = peer(d)
        there = got.at[p, pl.ds(10 * k, 10)]
        return remote(there, there, fs.at[p, k], fr.at[p, k], {"trc": k})

    def own(p):
        rows = pl.ds(pl.multiple_of(halves[p], 8), 8)
        return pltpu.make_async_copy(x_ref.at[:, me, rows], got.at[p, pl.ds(10 * me, 10)], fl.at[p])

    for p in range(2):
        for d in range(1, 8):
            forward(p, d).start()
        own(p).start()

    for load in loads[1:]:
        load.wait()
    species = lax.broadcasted_iota(jnp.int32, (80, 80), 1)
    held = column_of(v_as[...].astype(jnp.float32), 80).astype(jnp.int32)
    chosen = held == species
    pick = jnp.where(chosen, 1.0, 0.0).astype(jnp.bfloat16)
    first_w[...] = lax.dot_general(
        v_win[...], pick, (((1,), (1,)), ((), ())), preferred_element_type=jnp.float32
    ).astype(jnp.bfloat16)
    last_w[...] = jnp.dot(pick, v_wout[...], preferred_element_type=jnp.float32).astype(jnp.bfloat16)
    gain_b[...] = jnp.broadcast_to(jnp.sum(jnp.where(chosen, v_gain[...], 0.0), axis=1, keepdims=True), (80, 128))
    last_b[...] = jnp.broadcast_to(jnp.sum(jnp.where(chosen, v_bout[...], 0.0), axis=1, keepdims=True), (80, 128))
    bias_b[0] = jnp.broadcast_to(column_of(v_bin[...], 256), (256, 128))
    bias_b[1] = jnp.broadcast_to(column_of(v_bmid[0:1, :], 256), (256, 128))
    bias_b[2] = jnp.broadcast_to(column_of(v_bmid[1:2, :], 256), (256, 128))

    at_left = 0.5 * (pltpu.roll(c0, 1, 1) + c0)
    at_right = pltpu.roll(at_left, 127, 1)
    coef = upwind(at_right)[:3] + upwind(at_left)[3:]
    for i in range(6):
        cc[:, i, :] = coef[i]

    for copy in ec_copies:
        copy.wait()
    inner = lane8 % 16 < 8
    for side, wind8 in enumerate((jnp.where(inner, ecl[...], eco[...]), jnp.where(inner, eco[...], ecr[...]))):
        at_left = 0.5 * (pltpu.roll(wind8, 1, 1) + wind8)
        at_right = pltpu.roll(at_left, 127, 1)
        coef = upwind(at_right)[:3] + upwind(at_left)[3:]
        for i in range(6):
            sc[side, 0, i : i + 1, :] = coef[i][0:1]
            sc[side, 1, i : i + 1, :] = coef[i][1:2]

    @pl.when(y > 0)
    def _():
        wind_up.wait_send()
        wind_down.wait_recv()

    @pl.when(y < 3)
    def _():
        wind_down.wait_send()
        wind_up.wait_recv()

    c1 = cv[1]
    above = jnp.where(row16 == 0, c1h[0, 0:1, :], pltpu.roll(c1, 1, 0))
    coef = upwind(0.5 * (above + c1))
    for i in range(6):
        cf[0:16, i, :] = coef[i]
    coef = upwind(0.5 * (c1[15:16] + c1h[1, 0:1, :]))
    for i in range(6):
        cf[16, i : i + 1, :] = coef[i]

    got2 = [got.at[p].reshape(640, 128) for p in range(2)]
    back2 = [back.at[p].reshape(640, 128) for p in range(4)]

    def row_coef(ref, *at):
        return [ref[(*at, pl.ds(i, 1), slice(None))] for i in range(6)]

    def half(p):
        base = halves[p]
        for d in range(1, 8):
            arriving(p, d).wait_recv()
        own(p).wait()

        @pl.loop(0, 10)
        def _(g):
            e = jnp.zeros((8, 128), jnp.float32)
            for i in range(8):
                q = got2[p][pl.ds(g * 64 + i, 8, stride=8), :]
                e = jnp.where(lane8 // 16 == i, pltpu.roll(q, (16 * i + 8) % 128, 1), e)
            strip[p, pl.ds(pl.multiple_of(g * 8, 8), 8), :] = e

        for side, first in enumerate((8, 5)):
            for u in range(2):
                t = None
                for slot in range(5):
                    e = pltpu.roll(strip[p, 16 * slot + 8 * u : 16 * slot + 8 * u + 8, :], (3 * slot - first) % 128, 1)
                    t = e if t is None else jnp.where((lane8 % 16) // 3 == slot, e, t)
                t_out[p, side, 8 * u : 8 * u + 8, :] = t
        to_left = remote(t_out.at[p, 0], t_in.at[p, 1], ts.at[p, 0], tr.at[p, 1], left)
        to_right = remote(t_out.at[p, 1], t_in.at[p, 0], ts.at[p, 1], tr.at[p, 0], right)
        to_left.start()
        to_right.start()

        @pl.loop(0, 8)
        def _(i):
            coef = row_coef(cc, base + i)
            for g in range(0, 80, 16):
                q = got2[p][pl.ds(g * 8 + i, 16, stride=8), :]
                swept[base + i + 3, g : g + 16, :] = sweep_lanes(q, coef)

        to_left.wait()
        to_right.wait()
        coefs = [row_coef(sc, side, base // 8) for side in range(2)]
        for g in range(10):
            slot, u = g // 2, g % 2
            mine = strip[p, 8 * g : 8 * g + 8, :]
            before = pltpu.roll(t_in[p, 0, 8 * u : 8 * u + 8, :], (5 - 3 * slot) % 128, 1)
            after = pltpu.roll(t_in[p, 1, 8 * u : 8 * u + 8, :], (8 - 3 * slot) % 128, 1)
            new_left = sweep_lanes(jnp.where(inner, before, mine), coefs[0])
            new_right = sweep_lanes(jnp.where(inner, mine, after), coefs[1])
            fixed[8 * g : 8 * g + 8, :] = jnp.where(inner, new_right, new_left)
        sides = (lane8 < 3) | (lane8 >= 125)
        for i in range(8):
            for g in range(0, 80, 8):
                at = (base + i + 3, pl.ds(g, 8), slice(None))
                swept[at] = jnp.where(sides, pltpu.roll(fixed[g : g + 8, :], 120 - 16 * i, 1), swept[at])

    def rows_out(p):
        n = GROUPS[p]
        start = STARTS_ODD[p] + even * (STARTS_EVEN[p] - STARTS_ODD[p])

        @pl.loop(0, 10)
        def _(g):
            at = pl.ds(pl.multiple_of(g * 8, 8), 8)
            s = [swept[start + t, at, :] for t in range(n + 6)]
            e = [edge(*s[j : j + 4]) for j in range(n + 3)]
            flux = [None] * (n + 1)
            for j in range(n + 2):
                slope = e[j + 1] - e[j]
                curve = 6.0 * s[j + 2] - 3.0 * (e[j] + e[j + 1])
                if j <= n:
                    p1, p2, p3 = (cf[start + j, i : i + 1, :] for i in range(3))
                    flux[j] = p1 * e[j + 1] - p2 * slope + p3 * curve
                if j >= 1:
                    m1, m2, m3 = (cf[start + j - 1, i : i + 1, :] for i in range(3, 6))
                    flux[j - 1] = flux[j - 1] + (m1 * e[j] - m2 * slope - m3 * curve)
            for t in range(n):
                adv[t, at, :] = s[t + 3] - (flux[t + 1] - flux[t])

        wide = lambda v: jnp.concatenate([v] * n, axis=1)
        h = jnp.concatenate([(adv[t] * gain_b[...]).astype(jnp.bfloat16) for t in range(n)], axis=1)
        h = gelu(jnp.dot(first_w[...], h, preferred_element_type=jnp.float32) + wide(bias_b[0]))
        for m in range(2):
            h = gelu(jnp.dot(v_wmid[m], h, preferred_element_type=jnp.float32) + wide(bias_b[m + 1]))
        tend = jnp.dot(last_w[...], h, preferred_element_type=jnp.float32)
        for t in range(n):
            back2[p][pl.ds(t, 80, stride=8), :] = adv[t] + (tend[:, 128 * t : 128 * t + 128] + last_b[...])
        rows = pl.ds(start, n)
        for d in range(1, 8):
            k = peer(d)
            remote(
                back.at[p, pl.ds(10 * k, 10), pl.ds(0, n)], o_ref.at[:, me, rows], os_.at[p, k], or_.at[p, me], {"trc": k}
            ).start()
        pltpu.make_async_copy(back.at[p, pl.ds(10 * me, 10), pl.ds(0, n)], o_ref.at[:, me, rows], ol.at[p]).start()

    def finish(p):
        n = GROUPS[p]
        rows = pl.ds(STARTS_ODD[p] + even * (STARTS_EVEN[p] - STARTS_ODD[p]), n)
        for d in range(1, 8):
            k = peer(d)
            remote(
                back.at[p, pl.ds(10 * k, 10), pl.ds(0, n)], o_ref.at[:, k, rows], os_.at[p, k], or_.at[p, k], {"trc": k}
            ).wait()
        pltpu.make_async_copy(back.at[p, pl.ds(10 * me, 10), pl.ds(0, n)], o_ref.at[:, me, rows], ol.at[p]).wait()

    down = remote(swept.at[pl.ds(16, 3)], swept.at[pl.ds(0, 3)], hs.at[0], hr.at[0], {"ty": y + 1})
    up = remote(swept.at[pl.ds(3, 3)], swept.at[pl.ds(19, 3)], hs.at[1], hr.at[1], {"ty": y - 1})

    half(0)

    @pl.when(even == 1)
    def _():
        down.start()

    @pl.when(even == 0)
    def _():
        up.start()

    @pl.when(even == 1)
    def _():
        up.wait_recv()

    @pl.when(even == 0)
    def _():
        down.wait_recv()

    rows_out(0)
    half(1)

    @pl.when((even == 1) & (y > 0))
    def _():
        up.start()

    @pl.when((even == 0) & (y < 3))
    def _():
        down.start()

    rows_out(1)
    rows_out(2)

    @pl.when((even == 1) & (y > 0))
    def _():
        down.wait_recv()

    @pl.when((even == 0) & (y < 3))
    def _():
        up.wait_recv()

    rows_out(3)

    @pl.when(y > 0)
    def _():
        up.wait_send()

    @pl.when(y < 3)
    def _():
        down.wait_send()

    for p in range(2):
        for d in range(1, 8):
            forward(p, d).wait_send()
    for p in range(4):
        finish(p)


def local(tracers, courant, assignment, species_gain, w_in, b_in, w_mid, b_mid, w_out, b_out):
    f32, bf16 = jnp.float32, jnp.bfloat16
    dma = pltpu.SemaphoreType.DMA
    operands = (
        tracers, courant, assignment.reshape(1, 80), species_gain.reshape(1, 80), w_in, b_in.reshape(1, 256),
        w_mid, b_mid, w_out, b_out.reshape(1, 80),
    )
    scratch = [
        ((2, 80, 8, 128), f32), ((22, 80, 128), f32), ((2, 80, 128), f32), ((80, 128), f32), ((5, 80, 128), f32),
        ((4, 80, 8, 128), f32), ((2, 16, 128), f32), ((2, 8, 128), f32), ((8, 128), f32), ((8, 128), f32),
        ((8, 128), f32), ((2, 2, 16, 128), f32), ((2, 2, 16, 128), f32), ((16, 8, 128), f32), ((17, 8, 128), f32),
        ((2, 2, 8, 128), f32),
        ((1, 80), jnp.int32), ((1, 80), f32), ((256, 80), bf16), ((1, 256), f32), ((2, 256, 256), bf16),
        ((2, 256), f32), ((80, 256), bf16), ((1, 80), f32),
        ((256, 80), bf16), ((80, 256), bf16), ((3, 256, 128), f32), ((80, 128), f32), ((80, 128), f32),
    ]
    semaphores = [(2, 8), (2, 8), (2,), (9,), (2, 2), (2, 2), (2,), (2,), (2,), (2,), (2,), (2,), (4, 8), (4, 8), (4,)]
    return pl.pallas_call(
        kernel,
        out_shape=jax.ShapeDtypeStruct(tracers.shape, f32),
        in_specs=[pl.BlockSpec(memory_space=pl.ANY)] * len(operands),
        out_specs=pl.BlockSpec(memory_space=pl.ANY),
        scratch_shapes=[pltpu.VMEM(*s) for s in scratch] + [dma(s) for s in semaphores],
        compiler_params=pltpu.CompilerParams(
            collective_id=0, has_side_effects=True, vmem_limit_bytes=32 * 1024 * 1024
        ),
        cost_estimate=pl.CostEstimate(flops=704_000_000, bytes_accessed=4_000_000, transcendentals=1_600_000),
    )(*operands)


def solution(mesh):
    in_specs = (P("trc", None, "ty", "tx"), P(None, "trc", "ty", "tx")) + (P(),) * 8
    out_specs = P("trc", None, "ty", "tx")
    return jax.shard_map(local, mesh=mesh, in_specs=in_specs, out_specs=out_specs, check_vma=False)
```

```python
import functools

import jax
import jax.numpy as jnp
from jax import lax
from jax.experimental import pallas as pl
from jax.experimental.pallas import tpu as pltpu
from jax.sharding import PartitionSpec as P

MESH = pl.DeviceIdType.MESH
GROUPS = (2, 3, 4, 4, 3)
STARTS_EVEN = (11, 13, 7, 3, 0)
STARTS_ODD = (3, 0, 5, 9, 13)


def upwind(f):
    up, down = jnp.maximum(f, 0.0), jnp.minimum(f, 0.0)
    p2, m2 = 0.5 * up * up, 0.5 * down * down
    return up, p2, p2 * (1.0 - (2.0 / 3.0) * up), down, m2, m2 * (1.0 + (2.0 / 3.0) * down)


def edge(a, b, c, d):
    return (7.0 / 12.0) * (b + c) - (1.0 / 12.0) * (a + d)


def sweep_lanes(q, coef):
    p1, p2, p3, m1, m2, m3 = coef
    left = edge(pltpu.roll(q, 2, 1), pltpu.roll(q, 1, 1), q, pltpu.roll(q, 127, 1))
    right = pltpu.roll(left, 127, 1)
    slope = right - left
    curve = 6.0 * q - 3.0 * (left + right)
    out_right = p1 * right - p2 * slope + p3 * curve
    out_left = m1 * left - m2 * slope - m3 * curve
    return q - out_right + out_left + pltpu.roll(out_right, 1, 1) - pltpu.roll(out_left, 127, 1)


def gelu(v):
    inner = v * (0.7978845608028654 + (0.7978845608028654 * 0.044715) * (v * v))
    half = 0.5 * v
    return (half + half * jnp.tanh(inner)).astype(jnp.bfloat16)


def column_of(row, size):
    at = lax.broadcasted_iota(jnp.int32, (size, size), 0)
    to = lax.broadcasted_iota(jnp.int32, (size, size), 1)
    return jnp.sum(jnp.where(at == to, row, 0.0), axis=1, keepdims=True)


def kernel(
    x_ref, c_ref, as_ref, gain_ref, win_ref, bin_ref, wmid_ref, bmid_ref, wout_ref, bout_ref,
    o_ref,
    xv, got, swept, strip, fixed, adv, back, cv, c1h, eco, ecl, ecr, q_out, q_in, cc, cf, sc,
    v_as, v_gain, v_win, v_bin, v_wmid, v_bmid, v_wout, v_bout,
    first_w, last_w, bias_b, last_b, gain_b,
    fs, fr, fl, lw, qs, qr, ready, es, er, c1s, c1r, hs, hr, os_, or_, ol,
):
    me, y, x = lax.axis_index("trc"), lax.axis_index("ty"), lax.axis_index("tx")
    even = 1 - lax.rem(y, 2)
    left, right = {"tx": lax.rem(x + 15, 16)}, {"tx": lax.rem(x + 1, 16)}

    def remote(src, dst, send, recv, to):
        return pltpu.make_async_remote_copy(src, dst, send, recv, device_id=to, device_id_type=MESH)

    def peer(d):
        return lax.rem(me + d, 8)

    loads = [
        pltpu.make_async_copy(src, dst, lw.at[i])
        for i, (src, dst) in enumerate((
            (c_ref.at[:, 0], cv), (x_ref, xv), (as_ref, v_as), (gain_ref, v_gain), (win_ref, v_win), (bin_ref, v_bin),
            (wmid_ref, v_wmid), (bmid_ref, v_bmid), (wout_ref, v_wout), (bout_ref, v_bout),
        ))
    ]
    for load in loads:
        load.start()

    c1h[...] = jnp.zeros((2, 8, 128), jnp.float32)
    barrier = pltpu.get_barrier_semaphore()
    for d in range(1, 8):
        pl.semaphore_signal(barrier, inc=1, device_id={"trc": peer(d)}, device_id_type=MESH)
    for d in (1, 3):
        pl.semaphore_signal(barrier, inc=1, device_id={"ty": lax.rem(y + d, 4)}, device_id_type=MESH)

    first = lax.rem(x, 2) == 0

    @pl.when(first)
    def _():
        for side in (left, right):
            for k in range(8):
                pl.semaphore_signal(barrier, inc=1, device_id={"trc": k, **side}, device_id_type=MESH)

    lane8 = lax.broadcasted_iota(jnp.int32, (8, 128), 1)
    lane16 = lax.broadcasted_iota(jnp.int32, (16, 128), 1)
    row16 = lax.broadcasted_iota(jnp.int32, (16, 128), 0)

    loads[0].wait()
    c0 = cv[0]
    wind = jnp.zeros((16, 128), jnp.float32)
    for i in range(8):
        wind = jnp.where((lane16 // 16 == i) & (row16 % 8 == i), pltpu.roll(c0, (16 * i + 8) % 128, 1), wind)
    eco[...] = jnp.zeros((8, 128), jnp.float32)
    eco[0:1, :] = jnp.sum(wind[0:8], axis=0, keepdims=True)
    eco[1:2, :] = jnp.sum(wind[8:16], axis=0, keepdims=True)

    @pl.when(y == 0)
    def _():
        swept[0:3] = jnp.zeros((3, 80, 128), jnp.float32)

    @pl.when(y == 3)
    def _():
        swept[19:22] = jnp.zeros((3, 80, 128), jnp.float32)

    loads[1].wait()
    xv2 = xv.reshape(1280, 128)
    at16 = lane8 % 16

    @pl.loop(0, 10)
    def _(g):
        part = [jnp.zeros((8, 128), jnp.float32)] * 2
        for h in range(2):
            for i in range(8):
                v = pltpu.roll(xv2[pl.ds(g * 128 + 8 * h + i, 8, stride=16), :], (16 * i + 8) % 128, 1)
                part[h] = jnp.where(lane8 // 16 == i, v, part[h])
        q = jnp.where(at16 < 8, pltpu.roll(part[1], 125, 1), pltpu.roll(part[1], 3, 1))
        q_out[pl.ds(pl.multiple_of(g * 8, 8), 8), :] = jnp.where((at16 >= 5) & (at16 <= 10), part[0], q)

    q_out3 = q_out.reshape(10, 8, 128)

    def edges(side, k):
        return remote(
            q_out3.at[:, k], q_in.at[1 - side, pl.ds(10 * me, 10)], qs.at[side, k], qr.at[1 - side, me],
            {"trc": k, **(left, right)[side]},
        )

    ec_copies = (remote(eco, ecr, es.at[0], er.at[0], left), remote(eco, ecl, es.at[1], er.at[1], right))

    def send_edges():
        for copy in ec_copies:
            copy.start()
        for side in range(2):
            for k in range(8):
                edges(side, k).start()

    @pl.when(first)
    def _():
        pl.semaphore_wait(barrier, 9)

    @pl.when(jnp.logical_not(first))
    def _():
        pl.semaphore_wait(barrier, 25)
        for side in (left, right):
            for k in range(8):
                pl.semaphore_signal(ready, inc=1, device_id={"trc": k, **side}, device_id_type=MESH)
        send_edges()

    wind_up = remote(cv.at[1, pl.ds(0, 1)], c1h.at[1, pl.ds(0, 1)], c1s.at[0], c1r.at[0], {"ty": y - 1})
    wind_down = remote(cv.at[1, pl.ds(15, 1)], c1h.at[0, pl.ds(0, 1)], c1s.at[1], c1r.at[1], {"ty": y + 1})

    @pl.when(y > 0)
    def _():
        wind_up.start()

    @pl.when(y < 3)
    def _():
        wind_down.start()

    halves = (8 * even, 8 * (1 - even))

    def forward(p, d):
        k = peer(d)
        rows = pl.ds(pl.multiple_of(halves[p], 8), 8)
        return remote(
            x_ref.at[:, k, rows], got.at[p, pl.ds(10 * me, 10)], fs.at[p, k], fr.at[p, me], {"trc": k}
        )

    def arriving(p, d):
        k = peer(d)
        there = got.at[p, pl.ds(10 * k, 10)]
        return remote(there, there, fs.at[p, k], fr.at[p, k], {"trc": k})

    def own(p):
        rows = pl.ds(pl.multiple_of(halves[p], 8), 8)
        return pltpu.make_async_copy(x_ref.at[:, me, rows], got.at[p, pl.ds(10 * me, 10)], fl.at[p])

    for p in range(2):
        for d in range(1, 8):
            forward(p, d).start()
        own(p).start()

    for load in loads[2:]:
        load.wait()
    species = lax.broadcasted_iota(jnp.int32, (80, 80), 1)
    held = column_of(v_as[...].astype(jnp.float32), 80).astype(jnp.int32)
    chosen = held == species
    pick = jnp.where(chosen, 1.0, 0.0).astype(jnp.bfloat16)
    first_w[...] = lax.dot_general(
        v_win[...], pick, (((1,), (1,)), ((), ())), preferred_element_type=jnp.float32
    ).astype(jnp.bfloat16)
    last_w[...] = jnp.dot(pick, v_wout[...], preferred_element_type=jnp.float32).astype(jnp.bfloat16)
    gain_b[...] = jnp.broadcast_to(jnp.sum(jnp.where(chosen, v_gain[...], 0.0), axis=1, keepdims=True), (80, 128))
    last_b[...] = jnp.broadcast_to(jnp.sum(jnp.where(chosen, v_bout[...], 0.0), axis=1, keepdims=True), (80, 128))
    bias_b[0] = jnp.broadcast_to(column_of(v_bin[...], 256), (256, 128))
    bias_b[1] = jnp.broadcast_to(column_of(v_bmid[0:1, :], 256), (256, 128))
    bias_b[2] = jnp.broadcast_to(column_of(v_bmid[1:2, :], 256), (256, 128))

    at_left = 0.5 * (pltpu.roll(c0, 1, 1) + c0)
    at_right = pltpu.roll(at_left, 127, 1)
    coef = upwind(at_right)[:3] + upwind(at_left)[3:]
    for i in range(6):
        cc[:, i, :] = coef[i]

    @pl.when(first)
    def _():
        pl.semaphore_wait(ready, 16)
        send_edges()

    inner = lane8 % 16 < 8

    def strip_coefficients():
        for copy in ec_copies:
            copy.wait()
        for side in range(2):
            for k in range(8):
                there = q_in.at[1 - side, pl.ds(10 * k, 10)]
                remote(q_out3.at[:, k], there, qs.at[side, k], qr.at[1 - side, k], {"trc": k, **(left, right)[side]}).wait()
        winds = (jnp.where(inner, ecl[...], eco[...]), jnp.where(inner, eco[...], ecr[...]))
        for side, wind8 in enumerate(winds):
            at_left = 0.5 * (pltpu.roll(wind8, 1, 1) + wind8)
            at_right = pltpu.roll(at_left, 127, 1)
            coef = upwind(at_right)[:3] + upwind(at_left)[3:]
            for i in range(6):
                sc[side, 0, i : i + 1, :] = coef[i][0:1]
                sc[side, 1, i : i + 1, :] = coef[i][1:2]

    @pl.when(y > 0)
    def _():
        wind_up.wait_send()
        wind_down.wait_recv()

    @pl.when(y < 3)
    def _():
        wind_down.wait_send()
        wind_up.wait_recv()

    c1 = cv[1]
    above = jnp.where(row16 == 0, c1h[0, 0:1, :], pltpu.roll(c1, 1, 0))
    coef = upwind(0.5 * (above + c1))
    for i in range(6):
        cf[0:16, i, :] = coef[i]
    coef = upwind(0.5 * (c1[15:16] + c1h[1, 0:1, :]))
    for i in range(6):
        cf[16, i : i + 1, :] = coef[i]

    got2 = [got.at[p].reshape(640, 128) for p in range(2)]
    back2 = [back.at[p].reshape(640, 128) for p in range(5)]

    def row_coef(ref, *at):
        return [ref[(*at, pl.ds(i, 1), slice(None))] for i in range(6)]

    def half(p):
        base = halves[p]
        for d in range(1, 8):
            arriving(p, d).wait_recv()
        own(p).wait()

        @pl.loop(0, 10)
        def _(g):
            e = jnp.zeros((8, 128), jnp.float32)
            for i in range(8):
                q = got2[p][pl.ds(g * 64 + i, 8, stride=8), :]
                e = jnp.where(lane8 // 16 == i, pltpu.roll(q, (16 * i + 8) % 128, 1), e)
            strip[p, pl.ds(pl.multiple_of(g * 8, 8), 8), :] = e

        @pl.loop(0, 8)
        def _(i):
            coef = row_coef(cc, base + i)
            for g in range(0, 80, 16):
                q = got2[p][pl.ds(g * 8 + i, 16, stride=8), :]
                swept[base + i + 3, g : g + 16, :] = sweep_lanes(q, coef)

        if p == 0:
            strip_coefficients()
        coefs = [row_coef(sc, side, base // 8) for side in range(2)]
        h = base // 8
        for g in range(10):
            mine = strip[p, 8 * g : 8 * g + 8, :]
            before = pltpu.roll(q_in[0, 8 * g : 8 * g + 8, :], 3 * h, 1)
            after = pltpu.roll(q_in[1, 8 * g : 8 * g + 8, :], lax.rem(128 - 3 * h, 128), 1)
            new_left = sweep_lanes(jnp.where(inner, before, mine), coefs[0])
            new_right = sweep_lanes(jnp.where(inner, mine, after), coefs[1])
            fixed[8 * g : 8 * g + 8, :] = jnp.where(inner, new_right, new_left)
        sides = (lane8 < 3) | (lane8 >= 125)
        for i in range(8):
            for g in range(0, 80, 8):
                at = (base + i + 3, pl.ds(g, 8), slice(None))
                swept[at] = jnp.where(sides, pltpu.roll(fixed[g : g + 8, :], 120 - 16 * i, 1), swept[at])

    def rows_out(p):
        n = GROUPS[p]
        start = STARTS_ODD[p] + even * (STARTS_EVEN[p] - STARTS_ODD[p])

        @pl.loop(0, 10)
        def _(g):
            at = pl.ds(pl.multiple_of(g * 8, 8), 8)
            s = [swept[start + t, at, :] for t in range(n + 6)]
            e = [edge(*s[j : j + 4]) for j in range(n + 3)]
            flux = [None] * (n + 1)
            for j in range(n + 2):
                slope = e[j + 1] - e[j]
                curve = 6.0 * s[j + 2] - 3.0 * (e[j] + e[j + 1])
                if j <= n:
                    p1, p2, p3 = (cf[start + j, i : i + 1, :] for i in range(3))
                    flux[j] = p1 * e[j + 1] - p2 * slope + p3 * curve
                if j >= 1:
                    m1, m2, m3 = (cf[start + j - 1, i : i + 1, :] for i in range(3, 6))
                    flux[j - 1] = flux[j - 1] + (m1 * e[j] - m2 * slope - m3 * curve)
            for t in range(n):
                adv[t, at, :] = s[t + 3] - (flux[t + 1] - flux[t])

        wide = lambda v: jnp.concatenate([v] * n, axis=1)
        h = jnp.concatenate([(adv[t] * gain_b[...]).astype(jnp.bfloat16) for t in range(n)], axis=1)
        h = gelu(jnp.dot(first_w[...], h, preferred_element_type=jnp.float32) + wide(bias_b[0]))
        for m in range(2):
            h = gelu(jnp.dot(v_wmid[m], h, preferred_element_type=jnp.float32) + wide(bias_b[m + 1]))
        tend = jnp.dot(last_w[...], h, preferred_element_type=jnp.float32)
        for t in range(n):
            back2[p][pl.ds(t, 80, stride=8), :] = adv[t] + (tend[:, 128 * t : 128 * t + 128] + last_b[...])
        rows = pl.ds(start, n)
        for d in range(1, 8):
            k = peer(d)
            remote(
                back.at[p, pl.ds(10 * k, 10), pl.ds(0, n)], o_ref.at[:, me, rows], os_.at[p, k], or_.at[p, me], {"trc": k}
            ).start()
        pltpu.make_async_copy(back.at[p, pl.ds(10 * me, 10), pl.ds(0, n)], o_ref.at[:, me, rows], ol.at[p]).start()

    def finish(p):
        n = GROUPS[p]
        rows = pl.ds(STARTS_ODD[p] + even * (STARTS_EVEN[p] - STARTS_ODD[p]), n)
        for d in range(1, 8):
            k = peer(d)
            remote(
                back.at[p, pl.ds(10 * k, 10), pl.ds(0, n)], o_ref.at[:, k, rows], os_.at[p, k], or_.at[p, k], {"trc": k}
            ).wait()
        pltpu.make_async_copy(back.at[p, pl.ds(10 * me, 10), pl.ds(0, n)], o_ref.at[:, me, rows], ol.at[p]).wait()

    down = remote(swept.at[pl.ds(16, 3)], swept.at[pl.ds(0, 3)], hs.at[0], hr.at[0], {"ty": y + 1})
    up = remote(swept.at[pl.ds(3, 3)], swept.at[pl.ds(19, 3)], hs.at[1], hr.at[1], {"ty": y - 1})

    half(0)

    @pl.when(even == 1)
    def _():
        down.start()

    @pl.when(even == 0)
    def _():
        up.start()

    rows_out(0)

    @pl.when(even == 1)
    def _():
        up.wait_recv()

    @pl.when(even == 0)
    def _():
        down.wait_recv()

    rows_out(1)
    half(1)

    @pl.when((even == 1) & (y > 0))
    def _():
        up.start()

    @pl.when((even == 0) & (y < 3))
    def _():
        down.start()

    rows_out(2)
    rows_out(3)

    @pl.when((even == 1) & (y > 0))
    def _():
        down.wait_recv()

    @pl.when((even == 0) & (y < 3))
    def _():
        up.wait_recv()

    rows_out(4)

    @pl.when(y > 0)
    def _():
        up.wait_send()

    @pl.when(y < 3)
    def _():
        down.wait_send()

    for p in range(2):
        for d in range(1, 8):
            forward(p, d).wait_send()
    for p in range(5):
        finish(p)


def local(tracers, courant, assignment, species_gain, w_in, b_in, w_mid, b_mid, w_out, b_out):
    f32, bf16 = jnp.float32, jnp.bfloat16
    dma = pltpu.SemaphoreType.DMA
    operands = (
        tracers, courant, assignment.reshape(1, 80), species_gain.reshape(1, 80), w_in, b_in.reshape(1, 256),
        w_mid, b_mid, w_out, b_out.reshape(1, 80),
    )
    scratch = [
        ((10, 8, 16, 128), f32), ((2, 80, 8, 128), f32), ((22, 80, 128), f32), ((2, 80, 128), f32), ((80, 128), f32), ((5, 80, 128), f32),
        ((5, 80, 8, 128), f32), ((2, 16, 128), f32), ((2, 8, 128), f32), ((8, 128), f32), ((8, 128), f32),
        ((8, 128), f32), ((80, 128), f32), ((2, 80, 128), f32), ((16, 8, 128), f32), ((17, 8, 128), f32),
        ((2, 2, 8, 128), f32),
        ((1, 80), jnp.int32), ((1, 80), f32), ((256, 80), bf16), ((1, 256), f32), ((2, 256, 256), bf16),
        ((2, 256), f32), ((80, 256), bf16), ((1, 80), f32),
        ((256, 80), bf16), ((80, 256), bf16), ((3, 256, 128), f32), ((80, 128), f32), ((80, 128), f32),
    ]
    semaphores = [
        dma((2, 8)), dma((2, 8)), dma((2,)), dma((10,)), dma((2, 8)), dma((2, 8)), pltpu.SemaphoreType.REGULAR,
        dma((2,)), dma((2,)), dma((2,)), dma((2,)), dma((2,)), dma((2,)), dma((5, 8)), dma((5, 8)), dma((5,)),
    ]
    return pl.pallas_call(
        kernel,
        out_shape=jax.ShapeDtypeStruct(tracers.shape, f32),
        in_specs=[pl.BlockSpec(memory_space=pl.ANY)] * len(operands),
        out_specs=pl.BlockSpec(memory_space=pl.ANY),
        scratch_shapes=[pltpu.VMEM(*s) for s in scratch] + semaphores,
        compiler_params=pltpu.CompilerParams(
            collective_id=0, has_side_effects=True, vmem_limit_bytes=32 * 1024 * 1024
        ),
        cost_estimate=pl.CostEstimate(flops=704_000_000, bytes_accessed=4_000_000, transcendentals=1_600_000),
    )(*operands)


def solution(mesh):
    in_specs = (P("trc", None, "ty", "tx"), P(None, "trc", "ty", "tx")) + (P(),) * 8
    out_specs = P("trc", None, "ty", "tx")
    return jax.shard_map(local, mesh=mesh, in_specs=in_specs, out_specs=out_specs, check_vma=False)
```

```python
import functools

import jax
import jax.numpy as jnp
from jax import lax
from jax.experimental import pallas as pl
from jax.experimental.pallas import tpu as pltpu
from jax.sharding import PartitionSpec as P

MESH = pl.DeviceIdType.MESH
GROUPS = (2, 3, 4, 4, 3)
STARTS_EVEN = (11, 13, 7, 3, 0)
STARTS_ODD = (3, 0, 5, 9, 13)


def upwind(f):
    up, down = jnp.maximum(f, 0.0), jnp.minimum(f, 0.0)
    p2, m2 = 0.5 * up * up, 0.5 * down * down
    return up, p2, p2 * (1.0 - (2.0 / 3.0) * up), down, m2, m2 * (1.0 + (2.0 / 3.0) * down)


def edge(a, b, c, d):
    return (7.0 / 12.0) * (b + c) - (1.0 / 12.0) * (a + d)


def sweep_lanes(q, coef):
    p1, p2, p3, m1, m2, m3 = coef
    left = edge(pltpu.roll(q, 2, 1), pltpu.roll(q, 1, 1), q, pltpu.roll(q, 127, 1))
    right = pltpu.roll(left, 127, 1)
    slope = right - left
    curve = 6.0 * q - 3.0 * (left + right)
    out_right = p1 * right - p2 * slope + p3 * curve
    out_left = m1 * left - m2 * slope - m3 * curve
    return q - out_right + out_left + pltpu.roll(out_right, 1, 1) - pltpu.roll(out_left, 127, 1)


def gelu(v):
    inner = v * (0.7978845608028654 + (0.7978845608028654 * 0.044715) * (v * v))
    half = 0.5 * v
    return (half + half * jnp.tanh(inner)).astype(jnp.bfloat16)


def column_of(row, size):
    at = lax.broadcasted_iota(jnp.int32, (size, size), 0)
    to = lax.broadcasted_iota(jnp.int32, (size, size), 1)
    return jnp.sum(jnp.where(at == to, row, 0.0), axis=1, keepdims=True)


def kernel(
    x_ref, c_ref, as_ref, gain_ref, win_ref, bin_ref, wmid_ref, bmid_ref, wout_ref, bout_ref,
    o_ref,
    xv, got, swept, strip, fixed, adv, back, cv, c1h, eco, ecl, ecr, q_out, q_in, cc, cf, sc,
    v_as, v_gain, v_win, v_bin, v_wmid, v_bmid, v_wout, v_bout,
    first_w, last_w, bias_b, last_b, gain_b,
    fs, fr, fl, lw, qs, qr, ready, es, er, c1s, c1r, hs, hr, os_, or_, ol,
):
    me, y, x = lax.axis_index("trc"), lax.axis_index("ty"), lax.axis_index("tx")
    even = 1 - lax.rem(y, 2)
    left, right = {"tx": lax.rem(x + 15, 16)}, {"tx": lax.rem(x + 1, 16)}

    def remote(src, dst, send, recv, to):
        return pltpu.make_async_remote_copy(src, dst, send, recv, device_id=to, device_id_type=MESH)

    def peer(d):
        return lax.rem(me + d, 8)

    loads = [
        pltpu.make_async_copy(src, dst, lw.at[i])
        for i, (src, dst) in enumerate((
            (c_ref.at[:, 0], cv), (x_ref, xv), (as_ref, v_as), (gain_ref, v_gain), (win_ref, v_win), (bin_ref, v_bin),
            (wmid_ref, v_wmid), (bmid_ref, v_bmid), (wout_ref, v_wout), (bout_ref, v_bout),
        ))
    ]
    for load in loads:
        load.start()

    c1h[...] = jnp.zeros((2, 8, 128), jnp.float32)
    barrier = pltpu.get_barrier_semaphore()
    for d in range(1, 8):
        pl.semaphore_signal(barrier, inc=1, device_id={"trc": peer(d)}, device_id_type=MESH)
    for d in (1, 3):
        pl.semaphore_signal(barrier, inc=1, device_id={"ty": lax.rem(y + d, 4)}, device_id_type=MESH)

    first = lax.rem(x, 2) == 0

    @pl.when(first)
    def _():
        for side in (left, right):
            for k in range(8):
                pl.semaphore_signal(barrier, inc=1, device_id={"trc": k, **side}, device_id_type=MESH)

    lane8 = lax.broadcasted_iota(jnp.int32, (8, 128), 1)
    lane16 = lax.broadcasted_iota(jnp.int32, (16, 128), 1)
    row16 = lax.broadcasted_iota(jnp.int32, (16, 128), 0)

    loads[0].wait()
    c0 = cv[0]
    wind = jnp.zeros((16, 128), jnp.float32)
    for i in range(8):
        wind = jnp.where((lane16 // 16 == i) & (row16 % 8 == i), pltpu.roll(c0, (16 * i + 8) % 128, 1), wind)
    eco[...] = jnp.zeros((8, 128), jnp.float32)
    eco[0:1, :] = jnp.sum(wind[0:8], axis=0, keepdims=True)
    eco[1:2, :] = jnp.sum(wind[8:16], axis=0, keepdims=True)

    @pl.when(y == 0)
    def _():
        swept[0:3] = jnp.zeros((3, 80, 128), jnp.float32)

    @pl.when(y == 3)
    def _():
        swept[19:22] = jnp.zeros((3, 80, 128), jnp.float32)

    halves = (8 * even, 8 * (1 - even))

    def forward(p, d):
        k = peer(d)
        rows = pl.ds(pl.multiple_of(halves[p], 8), 8)
        return remote(
            x_ref.at[:, k, rows], got.at[p, pl.ds(10 * me, 10)], fs.at[p, k], fr.at[p, me], {"trc": k}
        )

    def arriving(p, d):
        k = peer(d)
        there = got.at[p, pl.ds(10 * k, 10)]
        return remote(there, there, fs.at[p, k], fr.at[p, k], {"trc": k})

    def own(p):
        rows = pl.ds(pl.multiple_of(halves[p], 8), 8)
        return pltpu.make_async_copy(x_ref.at[:, me, rows], got.at[p, pl.ds(10 * me, 10)], fl.at[p])

    loads[1].wait()
    xv2 = xv.reshape(1280, 128)
    at16 = lane8 % 16

    @pl.loop(0, 10, unroll=5)
    def _(g):
        part = [jnp.zeros((8, 128), jnp.float32)] * 2
        for h in range(2):
            for i in range(8):
                v = pltpu.roll(xv2[pl.ds(g * 128 + 8 * h + i, 8, stride=16), :], (16 * i + 8) % 128, 1)
                part[h] = jnp.where(lane8 // 16 == i, v, part[h])
        q = jnp.where(at16 < 8, pltpu.roll(part[1], 125, 1), pltpu.roll(part[1], 3, 1))
        q_out[pl.ds(pl.multiple_of(g * 8, 8), 8), :] = jnp.where((at16 >= 5) & (at16 <= 10), part[0], q)

    q_out3 = q_out.reshape(10, 8, 128)

    def edges(side, k):
        return remote(
            q_out3.at[:, k], q_in.at[1 - side, pl.ds(10 * me, 10)], qs.at[side, k], qr.at[1 - side, me],
            {"trc": k, **(left, right)[side]},
        )

    ec_copies = (remote(eco, ecr, es.at[0], er.at[0], left), remote(eco, ecl, es.at[1], er.at[1], right))

    def send_edges(side):
        ec_copies[side].start()
        for k in range(8):
            edges(side, k).start()

    def send_half(p):
        for d in range(1, 8):
            forward(p, d).start()
        own(p).start()

    def greeted(side):
        pl.semaphore_wait(ready.at[side], 8)

    @pl.when(first)
    def _():
        pl.semaphore_wait(barrier, 9)
        send_half(0)
        greeted(1)
        send_edges(1)

        @pl.when(x > 0)
        def _():
            greeted(0)
            send_edges(0)

        send_half(1)

    @pl.when(jnp.logical_not(first))
    def _():
        pl.semaphore_wait(barrier, 25)
        send_edges(1)
        for side, to in enumerate((left, right)):
            for k in range(8):
                pl.semaphore_signal(ready.at[1 - side], inc=1, device_id={"trc": k, **to}, device_id_type=MESH)
        send_edges(0)
        send_half(0)
        send_half(1)

    wind_up = remote(cv.at[1, pl.ds(0, 1)], c1h.at[1, pl.ds(0, 1)], c1s.at[0], c1r.at[0], {"ty": y - 1})
    wind_down = remote(cv.at[1, pl.ds(15, 1)], c1h.at[0, pl.ds(0, 1)], c1s.at[1], c1r.at[1], {"ty": y + 1})

    @pl.when(y > 0)
    def _():
        wind_up.start()

    @pl.when(y < 3)
    def _():
        wind_down.start()

    for load in loads[2:]:
        load.wait()
    species = lax.broadcasted_iota(jnp.int32, (80, 80), 1)
    held = column_of(v_as[...].astype(jnp.float32), 80).astype(jnp.int32)
    chosen = held == species
    pick = jnp.where(chosen, 1.0, 0.0).astype(jnp.bfloat16)
    first_w[...] = lax.dot_general(
        v_win[...], pick, (((1,), (1,)), ((), ())), preferred_element_type=jnp.float32
    ).astype(jnp.bfloat16)
    last_w[...] = jnp.dot(pick, v_wout[...], preferred_element_type=jnp.float32).astype(jnp.bfloat16)
    gain_b[...] = jnp.broadcast_to(jnp.sum(jnp.where(chosen, v_gain[...], 0.0), axis=1, keepdims=True), (80, 128))
    last_b[...] = jnp.broadcast_to(jnp.sum(jnp.where(chosen, v_bout[...], 0.0), axis=1, keepdims=True), (80, 128))
    bias_b[0] = jnp.broadcast_to(column_of(v_bin[...], 256), (256, 128))
    bias_b[1] = jnp.broadcast_to(column_of(v_bmid[0:1, :], 256), (256, 128))
    bias_b[2] = jnp.broadcast_to(column_of(v_bmid[1:2, :], 256), (256, 128))

    at_left = 0.5 * (pltpu.roll(c0, 1, 1) + c0)
    at_right = pltpu.roll(at_left, 127, 1)
    coef = upwind(at_right)[:3] + upwind(at_left)[3:]
    for i in range(6):
        cc[:, i, :] = coef[i]

    @pl.when(x == 0)
    def _():
        greeted(0)
        send_edges(0)

    inner = lane8 % 16 < 8

    def strip_coefficients():
        for copy in ec_copies:
            copy.wait_recv()
        for side in range(2):
            for k in range(8):
                there = q_in.at[side, pl.ds(10 * k, 10)]
                remote(there, there, qs.at[side, k], qr.at[side, k], {"trc": k, **(left, right)[side]}).wait_recv()
        winds = (jnp.where(inner, ecl[...], eco[...]), jnp.where(inner, eco[...], ecr[...]))
        for side, wind8 in enumerate(winds):
            at_left = 0.5 * (pltpu.roll(wind8, 1, 1) + wind8)
            at_right = pltpu.roll(at_left, 127, 1)
            coef = upwind(at_right)[:3] + upwind(at_left)[3:]
            for i in range(6):
                sc[side, 0, i : i + 1, :] = coef[i][0:1]
                sc[side, 1, i : i + 1, :] = coef[i][1:2]

    @pl.when(y > 0)
    def _():
        wind_up.wait_send()
        wind_down.wait_recv()

    @pl.when(y < 3)
    def _():
        wind_down.wait_send()
        wind_up.wait_recv()

    c1 = cv[1]
    above = jnp.where(row16 == 0, c1h[0, 0:1, :], pltpu.roll(c1, 1, 0))
    coef = upwind(0.5 * (above + c1))
    for i in range(6):
        cf[0:16, i, :] = coef[i]
    coef = upwind(0.5 * (c1[15:16] + c1h[1, 0:1, :]))
    for i in range(6):
        cf[16, i : i + 1, :] = coef[i]

    got2 = [got.at[p].reshape(640, 128) for p in range(2)]
    back2 = [back.at[p].reshape(640, 128) for p in range(5)]

    def row_coef(ref, *at):
        return [ref[(*at, pl.ds(i, 1), slice(None))] for i in range(6)]

    def half(p):
        base = halves[p]
        for d in range(1, 8):
            arriving(p, d).wait_recv()
        own(p).wait()

        @pl.loop(0, 10, unroll=5)
        def _(g):
            e = jnp.zeros((8, 128), jnp.float32)
            for i in range(8):
                q = got2[p][pl.ds(g * 64 + i, 8, stride=8), :]
                e = jnp.where(lane8 // 16 == i, pltpu.roll(q, (16 * i + 8) % 128, 1), e)
            strip[p, pl.ds(pl.multiple_of(g * 8, 8), 8), :] = e

        @pl.loop(0, 8, unroll=2)
        def _(i):
            coef = row_coef(cc, base + i)
            for g in range(0, 80, 16):
                q = got2[p][pl.ds(g * 8 + i, 16, stride=8), :]
                swept[base + i + 3, g : g + 16, :] = sweep_lanes(q, coef)

        if p == 0:
            strip_coefficients()
        coefs = [row_coef(sc, side, base // 8) for side in range(2)]
        h = base // 8
        for g in range(10):
            mine = strip[p, 8 * g : 8 * g + 8, :]
            before = pltpu.roll(q_in[0, 8 * g : 8 * g + 8, :], 3 * h, 1)
            after = pltpu.roll(q_in[1, 8 * g : 8 * g + 8, :], lax.rem(128 - 3 * h, 128), 1)
            new_left = sweep_lanes(jnp.where(inner, before, mine), coefs[0])
            new_right = sweep_lanes(jnp.where(inner, mine, after), coefs[1])
            fixed[8 * g : 8 * g + 8, :] = jnp.where(inner, new_right, new_left)
        sides = (lane8 < 3) | (lane8 >= 125)
        for i in range(8):
            for g in range(0, 80, 8):
                at = (base + i + 3, pl.ds(g, 8), slice(None))
                swept[at] = jnp.where(sides, pltpu.roll(fixed[g : g + 8, :], 120 - 16 * i, 1), swept[at])

    def rows_out(p):
        n = GROUPS[p]
        start = STARTS_ODD[p] + even * (STARTS_EVEN[p] - STARTS_ODD[p])

        @pl.loop(0, 10)
        def _(g):
            at = pl.ds(pl.multiple_of(g * 8, 8), 8)
            s = [swept[start + t, at, :] for t in range(n + 6)]
            e = [edge(*s[j : j + 4]) for j in range(n + 3)]
            flux = [None] * (n + 1)
            for j in range(n + 2):
                slope = e[j + 1] - e[j]
                curve = 6.0 * s[j + 2] - 3.0 * (e[j] + e[j + 1])
                if j <= n:
                    p1, p2, p3 = (cf[start + j, i : i + 1, :] for i in range(3))
                    flux[j] = p1 * e[j + 1] - p2 * slope + p3 * curve
                if j >= 1:
                    m1, m2, m3 = (cf[start + j - 1, i : i + 1, :] for i in range(3, 6))
                    flux[j - 1] = flux[j - 1] + (m1 * e[j] - m2 * slope - m3 * curve)
            for t in range(n):
                adv[t, at, :] = s[t + 3] - (flux[t + 1] - flux[t])

        wide = lambda v: jnp.concatenate([v] * n, axis=1)
        h = jnp.concatenate([(adv[t] * gain_b[...]).astype(jnp.bfloat16) for t in range(n)], axis=1)
        h = gelu(jnp.dot(first_w[...], h, preferred_element_type=jnp.float32) + wide(bias_b[0]))
        for m in range(2):
            h = gelu(jnp.dot(v_wmid[m], h, preferred_element_type=jnp.float32) + wide(bias_b[m + 1]))
        tend = jnp.dot(last_w[...], h, preferred_element_type=jnp.float32)
        for t in range(n):
            back2[p][pl.ds(t, 80, stride=8), :] = adv[t] + (tend[:, 128 * t : 128 * t + 128] + last_b[...])
        rows = pl.ds(start, n)
        for d in range(1, 8):
            k = peer(d)
            remote(
                back.at[p, pl.ds(10 * k, 10), pl.ds(0, n)], o_ref.at[:, me, rows], os_.at[p, k], or_.at[p, me], {"trc": k}
            ).start()
        pltpu.make_async_copy(back.at[p, pl.ds(10 * me, 10), pl.ds(0, n)], o_ref.at[:, me, rows], ol.at[p]).start()

    def finish(p):
        n = GROUPS[p]
        rows = pl.ds(STARTS_ODD[p] + even * (STARTS_EVEN[p] - STARTS_ODD[p]), n)
        for d in range(1, 8):
            k = peer(d)
            remote(
                back.at[p, pl.ds(10 * k, 10), pl.ds(0, n)], o_ref.at[:, k, rows], os_.at[p, k], or_.at[p, k], {"trc": k}
            ).wait()
        pltpu.make_async_copy(back.at[p, pl.ds(10 * me, 10), pl.ds(0, n)], o_ref.at[:, me, rows], ol.at[p]).wait()

    down = remote(swept.at[pl.ds(16, 3)], swept.at[pl.ds(0, 3)], hs.at[0], hr.at[0], {"ty": y + 1})
    up = remote(swept.at[pl.ds(3, 3)], swept.at[pl.ds(19, 3)], hs.at[1], hr.at[1], {"ty": y - 1})

    half(0)

    @pl.when(even == 1)
    def _():
        down.start()

    @pl.when(even == 0)
    def _():
        up.start()

    rows_out(0)

    @pl.when(even == 1)
    def _():
        up.wait_recv()

    @pl.when(even == 0)
    def _():
        down.wait_recv()

    rows_out(1)
    half(1)

    @pl.when((even == 1) & (y > 0))
    def _():
        up.start()

    @pl.when((even == 0) & (y < 3))
    def _():
        down.start()

    rows_out(2)
    rows_out(3)

    @pl.when((even == 1) & (y > 0))
    def _():
        down.wait_recv()

    @pl.when((even == 0) & (y < 3))
    def _():
        up.wait_recv()

    rows_out(4)

    @pl.when(y > 0)
    def _():
        up.wait_send()

    @pl.when(y < 3)
    def _():
        down.wait_send()

    for side in range(2):
        ec_copies[side].wait_send()
        for k in range(8):
            edges(side, k).wait_send()
    for p in range(2):
        for d in range(1, 8):
            forward(p, d).wait_send()
    for p in range(5):
        finish(p)


def local(tracers, courant, assignment, species_gain, w_in, b_in, w_mid, b_mid, w_out, b_out):
    f32, bf16 = jnp.float32, jnp.bfloat16
    dma = pltpu.SemaphoreType.DMA
    operands = (
        tracers, courant, assignment.reshape(1, 80), species_gain.reshape(1, 80), w_in, b_in.reshape(1, 256),
        w_mid, b_mid, w_out, b_out.reshape(1, 80),
    )
    scratch = [
        ((10, 8, 16, 128), f32), ((2, 80, 8, 128), f32), ((22, 80, 128), f32), ((2, 80, 128), f32), ((80, 128), f32), ((5, 80, 128), f32),
        ((5, 80, 8, 128), f32), ((2, 16, 128), f32), ((2, 8, 128), f32), ((8, 128), f32), ((8, 128), f32),
        ((8, 128), f32), ((80, 128), f32), ((2, 80, 128), f32), ((16, 8, 128), f32), ((17, 8, 128), f32),
        ((2, 2, 8, 128), f32),
        ((1, 80), jnp.int32), ((1, 80), f32), ((256, 80), bf16), ((1, 256), f32), ((2, 256, 256), bf16),
        ((2, 256), f32), ((80, 256), bf16), ((1, 80), f32),
        ((256, 80), bf16), ((80, 256), bf16), ((3, 256, 128), f32), ((80, 128), f32), ((80, 128), f32),
    ]
    semaphores = [
        dma((2, 8)), dma((2, 8)), dma((2,)), dma((10,)), dma((2, 8)), dma((2, 8)), pltpu.SemaphoreType.REGULAR((2,)),
        dma((2,)), dma((2,)), dma((2,)), dma((2,)), dma((2,)), dma((2,)), dma((5, 8)), dma((5, 8)), dma((5,)),
    ]
    return pl.pallas_call(
        kernel,
        out_shape=jax.ShapeDtypeStruct(tracers.shape, f32),
        in_specs=[pl.BlockSpec(memory_space=pl.ANY)] * len(operands),
        out_specs=pl.BlockSpec(memory_space=pl.ANY),
        scratch_shapes=[pltpu.VMEM(*s) for s in scratch] + semaphores,
        compiler_params=pltpu.CompilerParams(
            collective_id=0, has_side_effects=True, vmem_limit_bytes=32 * 1024 * 1024
        ),
        cost_estimate=pl.CostEstimate(flops=704_000_000, bytes_accessed=4_000_000, transcendentals=1_600_000),
    )(*operands)


def solution(mesh):
    in_specs = (P("trc", None, "ty", "tx"), P(None, "trc", "ty", "tx")) + (P(),) * 8
    out_specs = P("trc", None, "ty", "tx")
    return jax.shard_map(local, mesh=mesh, in_specs=in_specs, out_specs=out_specs, check_vma=False)
```

```python
import functools

import jax
import jax.numpy as jnp
from jax import lax
from jax.experimental import pallas as pl
from jax.experimental.pallas import tpu as pltpu
from jax.sharding import PartitionSpec as P

MESH = pl.DeviceIdType.MESH
VM = 60 * 1024 * 1024
GROUPS = (2, 3, 4, 4, 3)
STARTS_EVEN = (11, 13, 7, 3, 0)
STARTS_ODD = (3, 0, 5, 9, 13)


def upwind(f):
    up, down = jnp.maximum(f, 0.0), jnp.minimum(f, 0.0)
    p2, m2 = 0.5 * up * up, 0.5 * down * down
    return up, p2, p2 * (1.0 - (2.0 / 3.0) * up), down, m2, m2 * (1.0 + (2.0 / 3.0) * down)


def edge(a, b, c, d):
    return (7.0 / 12.0) * (b + c) - (1.0 / 12.0) * (a + d)


def sweep_lanes(q, coef):
    p1, p2, p3, m1, m2, m3 = coef
    left = edge(pltpu.roll(q, 2, 1), pltpu.roll(q, 1, 1), q, pltpu.roll(q, 127, 1))
    right = pltpu.roll(left, 127, 1)
    slope = right - left
    curve = 6.0 * q - 3.0 * (left + right)
    out_right = p1 * right - p2 * slope + p3 * curve
    out_left = m1 * left - m2 * slope - m3 * curve
    return q - out_right + out_left + pltpu.roll(out_right, 1, 1) - pltpu.roll(out_left, 127, 1)


def gelu(v):
    inner = v * (0.7978845608028654 + (0.7978845608028654 * 0.044715) * (v * v))
    half = 0.5 * v
    return (half + half * jnp.tanh(inner)).astype(jnp.bfloat16)


def column_of(row, size):
    at = lax.broadcasted_iota(jnp.int32, (size, size), 0)
    to = lax.broadcasted_iota(jnp.int32, (size, size), 1)
    return jnp.sum(jnp.where(at == to, row, 0.0), axis=1, keepdims=True)


def kernel(
    x_ref, c_ref, as_ref, gain_ref, win_ref, bin_ref, wmid_ref, bmid_ref, wout_ref, bout_ref,
    o_ref,
    xv, got, swept, strip, fixed, adv, back, cv, c1h, eco, ecl, ecr, q_out, q_in, cc, cf, sc,
    v_as, v_gain, v_win, v_bin, v_wmid, v_bmid, v_wout, v_bout,
    first_w, last_w, bias_b, last_b, gain_b,
    fs, fr, fl, lw, qs, qr, ready, es, er, c1s, c1r, hs, hr, os_, or_, ol,
):
    me, y, x = lax.axis_index("trc"), lax.axis_index("ty"), lax.axis_index("tx")
    even = 1 - lax.rem(y, 2)
    left, right = {"tx": lax.rem(x + 15, 16)}, {"tx": lax.rem(x + 1, 16)}

    def remote(src, dst, send, recv, to):
        return pltpu.make_async_remote_copy(src, dst, send, recv, device_id=to, device_id_type=MESH)

    def peer(d):
        return lax.rem(me + d, 8)

    loads = [
        pltpu.make_async_copy(src, dst, lw.at[i])
        for i, (src, dst) in enumerate((
            (c_ref.at[:, 0], cv), (x_ref, xv), (as_ref, v_as), (gain_ref, v_gain), (win_ref, v_win), (bin_ref, v_bin),
            (wmid_ref, v_wmid), (bmid_ref, v_bmid), (wout_ref, v_wout), (bout_ref, v_bout),
        ))
    ]
    for load in loads:
        load.start()

    c1h[...] = jnp.zeros((2, 8, 128), jnp.float32)
    barrier = pltpu.get_barrier_semaphore()
    for d in range(1, 8):
        pl.semaphore_signal(barrier, inc=1, device_id={"trc": peer(d)}, device_id_type=MESH)
    for d in (1, 3):
        pl.semaphore_signal(barrier, inc=1, device_id={"ty": lax.rem(y + d, 4)}, device_id_type=MESH)

    first = lax.rem(x, 2) == 0

    @pl.when(first)
    def _():
        for side in (left, right):
            for k in range(8):
                pl.semaphore_signal(barrier, inc=1, device_id={"trc": k, **side}, device_id_type=MESH)

    lane8 = lax.broadcasted_iota(jnp.int32, (8, 128), 1)
    lane16 = lax.broadcasted_iota(jnp.int32, (16, 128), 1)
    row16 = lax.broadcasted_iota(jnp.int32, (16, 128), 0)

    loads[0].wait()
    c0 = cv[0]
    wind = jnp.zeros((16, 128), jnp.float32)
    for i in range(8):
        wind = jnp.where((lane16 // 16 == i) & (row16 % 8 == i), pltpu.roll(c0, (16 * i + 8) % 128, 1), wind)
    eco[...] = jnp.zeros((8, 128), jnp.float32)
    eco[0:1, :] = jnp.sum(wind[0:8], axis=0, keepdims=True)
    eco[1:2, :] = jnp.sum(wind[8:16], axis=0, keepdims=True)

    @pl.when(y == 0)
    def _():
        swept[0:3] = jnp.zeros((3, 80, 128), jnp.float32)

    @pl.when(y == 3)
    def _():
        swept[19:22] = jnp.zeros((3, 80, 128), jnp.float32)

    halves = (8 * even, 8 * (1 - even))

    def forward(p, d):
        k = peer(d)
        rows = pl.ds(pl.multiple_of(halves[p], 8), 8)
        return remote(
            x_ref.at[:, k, rows], got.at[p, pl.ds(10 * me, 10)], fs.at[p, k], fr.at[p, me], {"trc": k}
        )

    def arriving(p, d):
        k = peer(d)
        there = got.at[p, pl.ds(10 * k, 10)]
        return remote(there, there, fs.at[p, k], fr.at[p, k], {"trc": k})

    def own(p):
        rows = pl.ds(pl.multiple_of(halves[p], 8), 8)
        return pltpu.make_async_copy(x_ref.at[:, me, rows], got.at[p, pl.ds(10 * me, 10)], fl.at[p])

    loads[1].wait()
    xv2 = xv.reshape(1280, 128)
    at16 = lane8 % 16

    @pl.loop(0, 10, unroll=5)
    def _(g):
        part = [jnp.zeros((8, 128), jnp.float32)] * 2
        for h in range(2):
            for i in range(8):
                v = pltpu.roll(xv2[pl.ds(g * 128 + 8 * h + i, 8, stride=16), :], (16 * i + 8) % 128, 1)
                part[h] = jnp.where(lane8 // 16 == i, v, part[h])
        q = jnp.where(at16 < 8, pltpu.roll(part[1], 125, 1), pltpu.roll(part[1], 3, 1))
        q_out[pl.ds(pl.multiple_of(g * 8, 8), 8), :] = jnp.where((at16 >= 5) & (at16 <= 10), part[0], q)

    q_out3 = q_out.reshape(10, 8, 128)

    def edges(side, k):
        return remote(
            q_out3.at[:, k], q_in.at[1 - side, pl.ds(10 * me, 10)], qs.at[side, k], qr.at[1 - side, me],
            {"trc": k, **(left, right)[side]},
        )

    ec_copies = (remote(eco, ecr, es.at[0], er.at[0], left), remote(eco, ecl, es.at[1], er.at[1], right))

    def send_edges(side):
        ec_copies[side].start()
        for k in range(8):
            edges(side, k).start()

    def send_half(p):
        for d in range(1, 8):
            forward(p, d).start()
        own(p).start()

    def greeted(side):
        pl.semaphore_wait(ready.at[side], 8)

    @pl.when(first)
    def _():
        pl.semaphore_wait(barrier, 9)
        send_half(0)
        greeted(1)
        send_edges(1)

        @pl.when(x > 0)
        def _():
            greeted(0)
            send_edges(0)

        send_half(1)

    @pl.when(jnp.logical_not(first))
    def _():
        pl.semaphore_wait(barrier, 25)
        for side, to in enumerate((left, right)):
            for k in range(8):
                pl.semaphore_signal(ready.at[1 - side], inc=1, device_id={"trc": k, **to}, device_id_type=MESH)
        send_edges(1)
        send_edges(0)
        send_half(0)
        send_half(1)

    wind_up = remote(cv.at[1, pl.ds(0, 1)], c1h.at[1, pl.ds(0, 1)], c1s.at[0], c1r.at[0], {"ty": y - 1})
    wind_down = remote(cv.at[1, pl.ds(15, 1)], c1h.at[0, pl.ds(0, 1)], c1s.at[1], c1r.at[1], {"ty": y + 1})

    @pl.when(y > 0)
    def _():
        wind_up.start()

    @pl.when(y < 3)
    def _():
        wind_down.start()

    for load in loads[2:]:
        load.wait()
    species = lax.broadcasted_iota(jnp.int32, (80, 80), 1)
    held = column_of(v_as[...].astype(jnp.float32), 80).astype(jnp.int32)
    chosen = held == species
    pick = jnp.where(chosen, 1.0, 0.0).astype(jnp.bfloat16)
    first_w[...] = lax.dot_general(
        v_win[...], pick, (((0,), (1,)), ((), ())), preferred_element_type=jnp.float32
    ).astype(jnp.bfloat16)
    last_w[...] = jnp.dot(pick, v_wout[...], preferred_element_type=jnp.float32).astype(jnp.bfloat16)
    gain_b[...] = jnp.broadcast_to(jnp.sum(jnp.where(chosen, v_gain[...], 0.0), axis=1, keepdims=True), (80, 128))
    last_b[...] = jnp.broadcast_to(jnp.sum(jnp.where(chosen, v_bout[...], 0.0), axis=1, keepdims=True), (80, 128))
    bias_b[0] = jnp.broadcast_to(column_of(v_bin[...], 256), (256, 128))
    bias_b[1] = jnp.broadcast_to(column_of(v_bmid[0:1, :], 256), (256, 128))
    bias_b[2] = jnp.broadcast_to(column_of(v_bmid[1:2, :], 256), (256, 128))

    at_left = 0.5 * (pltpu.roll(c0, 1, 1) + c0)
    at_right = pltpu.roll(at_left, 127, 1)
    coef = upwind(at_right)[:3] + upwind(at_left)[3:]
    for i in range(6):
        cc[:, i, :] = coef[i]

    @pl.when(x == 0)
    def _():
        greeted(0)
        send_edges(0)

    inner = lane8 % 16 < 8

    def strip_coefficients():
        for copy in ec_copies:
            copy.wait_recv()
        for side in range(2):
            for k in range(8):
                there = q_in.at[side, pl.ds(10 * k, 10)]
                remote(there, there, qs.at[side, k], qr.at[side, k], {"trc": k, **(left, right)[side]}).wait_recv()
        winds = (jnp.where(inner, ecl[...], eco[...]), jnp.where(inner, eco[...], ecr[...]))
        for side, wind8 in enumerate(winds):
            at_left = 0.5 * (pltpu.roll(wind8, 1, 1) + wind8)
            at_right = pltpu.roll(at_left, 127, 1)
            coef = upwind(at_right)[:3] + upwind(at_left)[3:]
            for i in range(6):
                sc[side, 0, i : i + 1, :] = coef[i][0:1]
                sc[side, 1, i : i + 1, :] = coef[i][1:2]

    @pl.when(y > 0)
    def _():
        wind_up.wait_send()
        wind_down.wait_recv()

    @pl.when(y < 3)
    def _():
        wind_down.wait_send()
        wind_up.wait_recv()

    c1 = cv[1]
    above = jnp.where(row16 == 0, c1h[0, 0:1, :], pltpu.roll(c1, 1, 0))
    coef = upwind(0.5 * (above + c1))
    for i in range(6):
        cf[0:16, i, :] = coef[i]
    coef = upwind(0.5 * (c1[15:16] + c1h[1, 0:1, :]))
    for i in range(6):
        cf[16, i : i + 1, :] = coef[i]

    got2 = [got.at[p].reshape(640, 128) for p in range(2)]
    back2 = [back.at[p].reshape(640, 128) for p in range(5)]

    def row_coef(ref, *at):
        return [ref[(*at, pl.ds(i, 1), slice(None))] for i in range(6)]

    def half(p):
        base = halves[p]
        for d in range(1, 8):
            arriving(p, d).wait_recv()
        own(p).wait()

        @pl.loop(0, 10, unroll=5)
        def _(g):
            e = jnp.zeros((8, 128), jnp.float32)
            for i in range(8):
                q = got2[p][pl.ds(g * 64 + i, 8, stride=8), :]
                e = jnp.where(lane8 // 16 == i, pltpu.roll(q, (16 * i + 8) % 128, 1), e)
            strip[p, pl.ds(pl.multiple_of(g * 8, 8), 8), :] = e

        @pl.loop(0, 8, unroll=2)
        def _(i):
            coef = row_coef(cc, base + i)
            for g in range(0, 80, 16):
                q = got2[p][pl.ds(g * 8 + i, 16, stride=8), :]
                swept[base + i + 3, g : g + 16, :] = sweep_lanes(q, coef)

        if p == 0:
            strip_coefficients()
        coefs = [row_coef(sc, side, base // 8) for side in range(2)]
        h = base // 8
        for g in range(10):
            mine = strip[p, 8 * g : 8 * g + 8, :]
            before = pltpu.roll(q_in[0, 8 * g : 8 * g + 8, :], 3 * h, 1)
            after = pltpu.roll(q_in[1, 8 * g : 8 * g + 8, :], lax.rem(128 - 3 * h, 128), 1)
            new_left = sweep_lanes(jnp.where(inner, before, mine), coefs[0])
            new_right = sweep_lanes(jnp.where(inner, mine, after), coefs[1])
            fixed[8 * g : 8 * g + 8, :] = jnp.where(inner, new_right, new_left)
        sides = (lane8 < 3) | (lane8 >= 125)
        for i in range(8):
            for g in range(0, 80, 8):
                at = (base + i + 3, pl.ds(g, 8), slice(None))
                swept[at] = jnp.where(sides, pltpu.roll(fixed[g : g + 8, :], 120 - 16 * i, 1), swept[at])

    def rows_out(p):
        n = GROUPS[p]
        start = STARTS_ODD[p] + even * (STARTS_EVEN[p] - STARTS_ODD[p])

        @pl.loop(0, 10)
        def _(g):
            at = pl.ds(pl.multiple_of(g * 8, 8), 8)
            s = [swept[start + t, at, :] for t in range(n + 6)]
            e = [edge(*s[j : j + 4]) for j in range(n + 3)]
            flux = [None] * (n + 1)
            for j in range(n + 2):
                slope = e[j + 1] - e[j]
                curve = 6.0 * s[j + 2] - 3.0 * (e[j] + e[j + 1])
                if j <= n:
                    p1, p2, p3 = (cf[start + j, i : i + 1, :] for i in range(3))
                    flux[j] = p1 * e[j + 1] - p2 * slope + p3 * curve
                if j >= 1:
                    m1, m2, m3 = (cf[start + j - 1, i : i + 1, :] for i in range(3, 6))
                    flux[j - 1] = flux[j - 1] + (m1 * e[j] - m2 * slope - m3 * curve)
            for t in range(n):
                adv[t, at, :] = s[t + 3] - (flux[t + 1] - flux[t])

        wide = lambda v: jnp.concatenate([v] * n, axis=1)
        h = jnp.concatenate([(adv[t] * gain_b[...]).astype(jnp.bfloat16) for t in range(n)], axis=1)
        h = gelu(jnp.dot(first_w[...], h, preferred_element_type=jnp.float32) + wide(bias_b[0]))
        for m in range(2):
            h = gelu(jnp.dot(v_wmid[m], h, preferred_element_type=jnp.float32) + wide(bias_b[m + 1]))
        tend = jnp.dot(last_w[...], h, preferred_element_type=jnp.float32)
        for t in range(n):
            back2[p][pl.ds(t, 80, stride=8), :] = adv[t] + (tend[:, 128 * t : 128 * t + 128] + last_b[...])
        rows = pl.ds(start, n)
        for d in range(1, 8):
            k = peer(d)
            remote(
                back.at[p, pl.ds(10 * k, 10), pl.ds(0, n)], o_ref.at[:, me, rows], os_.at[p, k], or_.at[p, me], {"trc": k}
            ).start()
        pltpu.make_async_copy(back.at[p, pl.ds(10 * me, 10), pl.ds(0, n)], o_ref.at[:, me, rows], ol.at[p]).start()

    def finish(p):
        n = GROUPS[p]
        rows = pl.ds(STARTS_ODD[p] + even * (STARTS_EVEN[p] - STARTS_ODD[p]), n)
        for d in range(1, 8):
            k = peer(d)
            remote(
                back.at[p, pl.ds(10 * k, 10), pl.ds(0, n)], o_ref.at[:, k, rows], os_.at[p, k], or_.at[p, k], {"trc": k}
            ).wait()
        pltpu.make_async_copy(back.at[p, pl.ds(10 * me, 10), pl.ds(0, n)], o_ref.at[:, me, rows], ol.at[p]).wait()

    down = remote(swept.at[pl.ds(16, 3)], swept.at[pl.ds(0, 3)], hs.at[0], hr.at[0], {"ty": y + 1})
    up = remote(swept.at[pl.ds(3, 3)], swept.at[pl.ds(19, 3)], hs.at[1], hr.at[1], {"ty": y - 1})

    half(0)

    @pl.when(even == 1)
    def _():
        down.start()

    @pl.when(even == 0)
    def _():
        up.start()

    rows_out(0)

    @pl.when(even == 1)
    def _():
        up.wait_recv()

    @pl.when(even == 0)
    def _():
        down.wait_recv()

    rows_out(1)
    half(1)

    @pl.when((even == 1) & (y > 0))
    def _():
        up.start()

    @pl.when((even == 0) & (y < 3))
    def _():
        down.start()

    rows_out(2)
    rows_out(3)

    @pl.when((even == 1) & (y > 0))
    def _():
        down.wait_recv()

    @pl.when((even == 0) & (y < 3))
    def _():
        up.wait_recv()

    rows_out(4)

    @pl.when(y > 0)
    def _():
        up.wait_send()

    @pl.when(y < 3)
    def _():
        down.wait_send()

    for side in range(2):
        ec_copies[side].wait_send()
        for k in range(8):
            edges(side, k).wait_send()
    for p in range(2):
        for d in range(1, 8):
            forward(p, d).wait_send()
    for p in range(5):
        finish(p)


def local(tracers, courant, assignment, species_gain, w_in, b_in, w_mid, b_mid, w_out, b_out):
    f32, bf16 = jnp.float32, jnp.bfloat16
    dma = pltpu.SemaphoreType.DMA
    operands = (
        tracers, courant, assignment.reshape(1, 80), species_gain.reshape(1, 80), w_in.T, b_in.reshape(1, 256),
        w_mid, b_mid, w_out, b_out.reshape(1, 80),
    )
    scratch = [
        ((10, 8, 16, 128), f32), ((2, 80, 8, 128), f32), ((22, 80, 128), f32), ((2, 80, 128), f32), ((80, 128), f32), ((5, 80, 128), f32),
        ((5, 80, 8, 128), f32), ((2, 16, 128), f32), ((2, 8, 128), f32), ((8, 128), f32), ((8, 128), f32),
        ((8, 128), f32), ((80, 128), f32), ((2, 80, 128), f32), ((16, 8, 128), f32), ((17, 8, 128), f32),
        ((2, 2, 8, 128), f32),
        ((1, 80), jnp.int32), ((1, 80), f32), ((80, 256), bf16), ((1, 256), f32), ((2, 256, 256), bf16),
        ((2, 256), f32), ((80, 256), bf16), ((1, 80), f32),
        ((256, 80), bf16), ((80, 256), bf16), ((3, 256, 128), f32), ((80, 128), f32), ((80, 128), f32),
    ]
    semaphores = [
        dma((2, 8)), dma((2, 8)), dma((2,)), dma((10,)), dma((2, 8)), dma((2, 8)), pltpu.SemaphoreType.REGULAR((2,)),
        dma((2,)), dma((2,)), dma((2,)), dma((2,)), dma((2,)), dma((2,)), dma((5, 8)), dma((5, 8)), dma((5,)),
    ]
    return pl.pallas_call(
        kernel,
        out_shape=jax.ShapeDtypeStruct(tracers.shape, f32),
        in_specs=[pl.BlockSpec(memory_space=pl.ANY)] * len(operands),
        out_specs=pl.BlockSpec(memory_space=pl.ANY),
        scratch_shapes=[pltpu.VMEM(*s) for s in scratch] + semaphores,
        compiler_params=pltpu.CompilerParams(
            collective_id=0, has_side_effects=True, vmem_limit_bytes=VM
        ),
        cost_estimate=pl.CostEstimate(flops=704_000_000, bytes_accessed=4_000_000, transcendentals=1_600_000),
    )(*operands)


def solution(mesh):
    in_specs = (P("trc", None, "ty", "tx"), P(None, "trc", "ty", "tx")) + (P(),) * 8
    out_specs = P("trc", None, "ty", "tx")
    return jax.shard_map(local, mesh=mesh, in_specs=in_specs, out_specs=out_specs, check_vma=False)
```

```python
import functools

import jax
import jax.numpy as jnp
from jax import lax
from jax.experimental import pallas as pl
from jax.experimental.pallas import tpu as pltpu
from jax.sharding import PartitionSpec as P

MESH = pl.DeviceIdType.MESH
VM = 60 * 1024 * 1024
GROUPS = (2, 3, 2, 6, 3)
STARTS_EVEN = (11, 13, 9, 3, 0)
STARTS_ODD = (3, 0, 5, 7, 13)


def upwind(f):
    up, down = jnp.maximum(f, 0.0), jnp.minimum(f, 0.0)
    p2, m2 = 0.5 * up * up, 0.5 * down * down
    return up, p2, p2 * (1.0 - (2.0 / 3.0) * up), down, m2, m2 * (1.0 + (2.0 / 3.0) * down)


def edge(a, b, c, d):
    return (7.0 / 12.0) * (b + c) - (1.0 / 12.0) * (a + d)


def sweep_lanes(q, coef):
    p1, p2, p3, m1, m2, m3 = coef
    left = edge(pltpu.roll(q, 2, 1), pltpu.roll(q, 1, 1), q, pltpu.roll(q, 127, 1))
    right = pltpu.roll(left, 127, 1)
    slope = right - left
    curve = 6.0 * q - 3.0 * (left + right)
    out_right = p1 * right - p2 * slope + p3 * curve
    out_left = m1 * left - m2 * slope - m3 * curve
    return q - out_right + out_left + pltpu.roll(out_right, 1, 1) - pltpu.roll(out_left, 127, 1)


def gelu(v):
    inner = v * (0.7978845608028654 + (0.7978845608028654 * 0.044715) * (v * v))
    half = 0.5 * v
    return (half + half * jnp.tanh(inner)).astype(jnp.bfloat16)


def column_of(row, size):
    at = lax.broadcasted_iota(jnp.int32, (size, size), 0)
    to = lax.broadcasted_iota(jnp.int32, (size, size), 1)
    return jnp.sum(jnp.where(at == to, row, 0.0), axis=1, keepdims=True)


def kernel(
    x_ref, c_ref, as_ref, gain_ref, win_ref, bin_ref, wmid_ref, bmid_ref, wout_ref, bout_ref,
    o_ref,
    xv, got, swept, strip, fixed, adv, back, cv, c1h, eco, ecl, ecr, q_out, q_in, cc, cf, sc,
    v_as, v_gain, v_win, v_bin, v_wmid, v_bmid, v_wout, v_bout,
    first_w, last_w, bias_b, last_b, gain_b,
    fs, fr, fl, lw, qs, qr, ready, es, er, c1s, c1r, hs, hr, os_, or_, ol,
):
    me, y, x = lax.axis_index("trc"), lax.axis_index("ty"), lax.axis_index("tx")
    even = 1 - lax.rem(y, 2)
    left, right = {"tx": lax.rem(x + 15, 16)}, {"tx": lax.rem(x + 1, 16)}

    def remote(src, dst, send, recv, to):
        return pltpu.make_async_remote_copy(src, dst, send, recv, device_id=to, device_id_type=MESH)

    def peer(d):
        return lax.rem(me + d, 8)

    loads = [
        pltpu.make_async_copy(src, dst, lw.at[i])
        for i, (src, dst) in enumerate((
            (c_ref.at[:, 0], cv), (x_ref, xv), (as_ref, v_as), (gain_ref, v_gain), (win_ref, v_win), (bin_ref, v_bin),
            (wmid_ref, v_wmid), (bmid_ref, v_bmid), (wout_ref, v_wout), (bout_ref, v_bout),
        ))
    ]
    for load in loads:
        load.start()

    c1h[...] = jnp.zeros((2, 8, 128), jnp.float32)
    barrier = pltpu.get_barrier_semaphore()
    first = lax.rem(x, 2) == 0

    @pl.when(first)
    def _():
        for side in (left, right):
            for k in range(8):
                pl.semaphore_signal(barrier, inc=1, device_id={"trc": k, **side}, device_id_type=MESH)

    for d in range(1, 8):
        pl.semaphore_signal(barrier, inc=1, device_id={"trc": peer(d)}, device_id_type=MESH)
    for d in (1, 3):
        pl.semaphore_signal(barrier, inc=1, device_id={"ty": lax.rem(y + d, 4)}, device_id_type=MESH)

    lane8 = lax.broadcasted_iota(jnp.int32, (8, 128), 1)
    lane16 = lax.broadcasted_iota(jnp.int32, (16, 128), 1)
    row16 = lax.broadcasted_iota(jnp.int32, (16, 128), 0)

    loads[0].wait()
    c0 = cv[0]
    wind = jnp.zeros((16, 128), jnp.float32)
    for i in range(8):
        wind = jnp.where((lane16 // 16 == i) & (row16 % 8 == i), pltpu.roll(c0, (16 * i + 8) % 128, 1), wind)
    eco[...] = jnp.zeros((8, 128), jnp.float32)
    eco[0:1, :] = jnp.sum(wind[0:8], axis=0, keepdims=True)
    eco[1:2, :] = jnp.sum(wind[8:16], axis=0, keepdims=True)

    @pl.when(y == 0)
    def _():
        swept[0:3] = jnp.zeros((3, 80, 128), jnp.float32)

    @pl.when(y == 3)
    def _():
        swept[19:22] = jnp.zeros((3, 80, 128), jnp.float32)

    halves = (8 * even, 8 * (1 - even))

    def forward(p, d):
        k = peer(d)
        rows = pl.ds(pl.multiple_of(halves[p], 8), 8)
        return remote(
            x_ref.at[:, k, rows], got.at[p, pl.ds(10 * me, 10)], fs.at[p, k], fr.at[p, me], {"trc": k}
        )

    def arriving(p, d):
        k = peer(d)
        there = got.at[p, pl.ds(10 * k, 10)]
        return remote(there, there, fs.at[p, k], fr.at[p, k], {"trc": k})

    def own(p):
        rows = pl.ds(pl.multiple_of(halves[p], 8), 8)
        return pltpu.make_async_copy(x_ref.at[:, me, rows], got.at[p, pl.ds(10 * me, 10)], fl.at[p])

    loads[1].wait()
    xv2 = xv.reshape(1280, 128)
    at16 = lane8 % 16

    @pl.loop(0, 10, unroll=5)
    def _(g):
        part = [jnp.zeros((8, 128), jnp.float32)] * 2
        for h in range(2):
            for i in range(8):
                v = pltpu.roll(xv2[pl.ds(g * 128 + 8 * h + i, 8, stride=16), :], (16 * i + 8) % 128, 1)
                part[h] = jnp.where(lane8 // 16 == i, v, part[h])
        q = jnp.where(at16 < 8, pltpu.roll(part[1], 125, 1), pltpu.roll(part[1], 3, 1))
        q_out[pl.ds(g, 8, stride=16), :] = jnp.where((at16 >= 5) & (at16 <= 10), part[0], q)

    q_out3 = q_out.reshape(8, 16, 128)

    def edges(side, k):
        return remote(
            q_out3.at[k, pl.ds(0, 10)], q_in.at[1 - side, pl.ds(10 * me, 10)], qs.at[side, k], qr.at[1 - side, me],
            {"trc": k, **(left, right)[side]},
        )

    ec_copies = (remote(eco, ecr, es.at[0], er.at[0], left), remote(eco, ecl, es.at[1], er.at[1], right))

    def send_edges(side):
        ec_copies[side].start()
        for k in range(8):
            edges(side, k).start()

    def send_half(p):
        for d in range(1, 8):
            forward(p, d).start()
        own(p).start()

    def greeted(side):
        pl.semaphore_wait(ready.at[side], 8)

    @pl.when(first)
    def _():
        pl.semaphore_wait(barrier, 9)
        send_half(0)
        greeted(1)
        send_edges(1)

        @pl.when(x > 0)
        def _():
            greeted(0)
            send_edges(0)

        send_half(1)

    @pl.when(jnp.logical_not(first))
    def _():
        pl.semaphore_wait(barrier, 25)
        for side, to in enumerate((left, right)):
            for k in range(8):
                pl.semaphore_signal(ready.at[1 - side], inc=1, device_id={"trc": k, **to}, device_id_type=MESH)
        send_edges(1)
        send_edges(0)
        send_half(0)
        send_half(1)

    wind_up = remote(cv.at[1, pl.ds(0, 1)], c1h.at[1, pl.ds(0, 1)], c1s.at[0], c1r.at[0], {"ty": y - 1})
    wind_down = remote(cv.at[1, pl.ds(15, 1)], c1h.at[0, pl.ds(0, 1)], c1s.at[1], c1r.at[1], {"ty": y + 1})

    @pl.when(y > 0)
    def _():
        wind_up.start()

    @pl.when(y < 3)
    def _():
        wind_down.start()

    for load in loads[2:]:
        load.wait()
    species = lax.broadcasted_iota(jnp.int32, (80, 80), 1)
    held = column_of(v_as[...].astype(jnp.float32), 80).astype(jnp.int32)
    chosen = held == species
    pick = jnp.where(chosen, 1.0, 0.0).astype(jnp.bfloat16)
    first_w[...] = lax.dot_general(
        v_win[...], pick, (((0,), (1,)), ((), ())), preferred_element_type=jnp.float32
    ).astype(jnp.bfloat16)
    last_w[...] = jnp.dot(pick, v_wout[...], preferred_element_type=jnp.float32).astype(jnp.bfloat16)
    gain_b[...] = jnp.broadcast_to(jnp.sum(jnp.where(chosen, v_gain[...], 0.0), axis=1, keepdims=True), (80, 128))
    last_b[...] = jnp.broadcast_to(jnp.sum(jnp.where(chosen, v_bout[...], 0.0), axis=1, keepdims=True), (80, 128))
    bias_b[0] = jnp.broadcast_to(column_of(v_bin[...], 256), (256, 128))
    bias_b[1] = jnp.broadcast_to(column_of(v_bmid[0:1, :], 256), (256, 128))
    bias_b[2] = jnp.broadcast_to(column_of(v_bmid[1:2, :], 256), (256, 128))

    at_left = 0.5 * (pltpu.roll(c0, 1, 1) + c0)
    at_right = pltpu.roll(at_left, 127, 1)
    coef = upwind(at_right)[:3] + upwind(at_left)[3:]
    for i in range(6):
        cc[:, i, :] = coef[i]

    @pl.when(x == 0)
    def _():
        greeted(0)
        send_edges(0)

    inner = lane8 % 16 < 8

    def strip_coefficients():
        for copy in ec_copies:
            copy.wait_recv()
        for side in range(2):
            for k in range(8):
                there = q_in.at[side, pl.ds(10 * k, 10)]
                remote(there, there, qs.at[side, k], qr.at[side, k], {"trc": k, **(left, right)[side]}).wait_recv()
        winds = (jnp.where(inner, ecl[...], eco[...]), jnp.where(inner, eco[...], ecr[...]))
        for side, wind8 in enumerate(winds):
            at_left = 0.5 * (pltpu.roll(wind8, 1, 1) + wind8)
            at_right = pltpu.roll(at_left, 127, 1)
            coef = upwind(at_right)[:3] + upwind(at_left)[3:]
            for i in range(6):
                sc[side, 0, i : i + 1, :] = coef[i][0:1]
                sc[side, 1, i : i + 1, :] = coef[i][1:2]

    @pl.when(y > 0)
    def _():
        wind_up.wait_send()
        wind_down.wait_recv()

    @pl.when(y < 3)
    def _():
        wind_down.wait_send()
        wind_up.wait_recv()

    c1 = cv[1]
    above = jnp.where(row16 == 0, c1h[0, 0:1, :], pltpu.roll(c1, 1, 0))
    coef = upwind(0.5 * (above + c1))
    for i in range(6):
        cf[0:16, i, :] = coef[i]
    coef = upwind(0.5 * (c1[15:16] + c1h[1, 0:1, :]))
    for i in range(6):
        cf[16, i : i + 1, :] = coef[i]

    got2 = [got.at[p].reshape(640, 128) for p in range(2)]
    back2 = [back.at[p].reshape(640, 128) for p in range(5)]

    def row_coef(ref, *at):
        return [ref[(*at, pl.ds(i, 1), slice(None))] for i in range(6)]

    def half(p):
        base = halves[p]
        for d in range(1, 8):
            arriving(p, d).wait_recv()
        own(p).wait()

        @pl.loop(0, 10, unroll=5)
        def _(g):
            e = jnp.zeros((8, 128), jnp.float32)
            for i in range(8):
                q = got2[p][pl.ds(g * 64 + i, 8, stride=8), :]
                e = jnp.where(lane8 // 16 == i, pltpu.roll(q, (16 * i + 8) % 128, 1), e)
            strip[p, pl.ds(pl.multiple_of(g * 8, 8), 8), :] = e

        @pl.loop(0, 8, unroll=2)
        def _(i):
            coef = row_coef(cc, base + i)
            for g in range(0, 80, 16):
                q = got2[p][pl.ds(g * 8 + i, 16, stride=8), :]
                swept[base + i + 3, g : g + 16, :] = sweep_lanes(q, coef)

        if p == 0:
            strip_coefficients()
        coefs = [row_coef(sc, side, base // 8) for side in range(2)]
        h = base // 8
        for g in range(10):
            mine = strip[p, 8 * g : 8 * g + 8, :]
            before = pltpu.roll(q_in[0, 8 * g : 8 * g + 8, :], 3 * h, 1)
            after = pltpu.roll(q_in[1, 8 * g : 8 * g + 8, :], lax.rem(128 - 3 * h, 128), 1)
            new_left = sweep_lanes(jnp.where(inner, before, mine), coefs[0])
            new_right = sweep_lanes(jnp.where(inner, mine, after), coefs[1])
            fixed[8 * g : 8 * g + 8, :] = jnp.where(inner, new_right, new_left)
        sides = (lane8 < 3) | (lane8 >= 125)
        for i in range(8):
            for g in range(0, 80, 8):
                at = (base + i + 3, pl.ds(g, 8), slice(None))
                swept[at] = jnp.where(sides, pltpu.roll(fixed[g : g + 8, :], 120 - 16 * i, 1), swept[at])

    def rows_out(p):
        n = GROUPS[p]
        start = STARTS_ODD[p] + even * (STARTS_EVEN[p] - STARTS_ODD[p])

        @pl.loop(0, 10, unroll=2)
        def _(g):
            at = pl.ds(pl.multiple_of(g * 8, 8), 8)
            s = [swept[start + t, at, :] for t in range(n + 6)]
            e = [edge(*s[j : j + 4]) for j in range(n + 3)]
            flux = [None] * (n + 1)
            for j in range(n + 2):
                slope = e[j + 1] - e[j]
                curve = 6.0 * s[j + 2] - 3.0 * (e[j] + e[j + 1])
                if j <= n:
                    p1, p2, p3 = (cf[start + j, i : i + 1, :] for i in range(3))
                    flux[j] = p1 * e[j + 1] - p2 * slope + p3 * curve
                if j >= 1:
                    m1, m2, m3 = (cf[start + j - 1, i : i + 1, :] for i in range(3, 6))
                    flux[j - 1] = flux[j - 1] + (m1 * e[j] - m2 * slope - m3 * curve)
            for t in range(n):
                adv[t, at, :] = s[t + 3] - (flux[t + 1] - flux[t])

        wide = lambda v: jnp.concatenate([v] * n, axis=1)
        h = jnp.concatenate([(adv[t] * gain_b[...]).astype(jnp.bfloat16) for t in range(n)], axis=1)
        h = gelu(jnp.dot(first_w[...], h, preferred_element_type=jnp.float32) + wide(bias_b[0]))
        for m in range(2):
            h = gelu(jnp.dot(v_wmid[m], h, preferred_element_type=jnp.float32) + wide(bias_b[m + 1]))
        tend = jnp.dot(last_w[...], h, preferred_element_type=jnp.float32)
        for t in range(n):
            back2[p][pl.ds(t, 80, stride=8), :] = adv[t] + (tend[:, 128 * t : 128 * t + 128] + last_b[...])
        rows = pl.ds(start, n)
        for d in range(1, 8):
            k = peer(d)
            remote(
                back.at[p, pl.ds(10 * k, 10), pl.ds(0, n)], o_ref.at[:, me, rows], os_.at[p, k], or_.at[p, me], {"trc": k}
            ).start()
        pltpu.make_async_copy(back.at[p, pl.ds(10 * me, 10), pl.ds(0, n)], o_ref.at[:, me, rows], ol.at[p]).start()

    def finish(p):
        n = GROUPS[p]
        rows = pl.ds(STARTS_ODD[p] + even * (STARTS_EVEN[p] - STARTS_ODD[p]), n)
        for d in range(1, 8):
            k = peer(d)
            remote(
                back.at[p, pl.ds(10 * k, 10), pl.ds(0, n)], o_ref.at[:, k, rows], os_.at[p, k], or_.at[p, k], {"trc": k}
            ).wait()
        pltpu.make_async_copy(back.at[p, pl.ds(10 * me, 10), pl.ds(0, n)], o_ref.at[:, me, rows], ol.at[p]).wait()

    down = remote(swept.at[pl.ds(16, 3)], swept.at[pl.ds(0, 3)], hs.at[0], hr.at[0], {"ty": y + 1})
    up = remote(swept.at[pl.ds(3, 3)], swept.at[pl.ds(19, 3)], hs.at[1], hr.at[1], {"ty": y - 1})

    half(0)

    @pl.when(even == 1)
    def _():
        down.start()

    @pl.when(even == 0)
    def _():
        up.start()

    rows_out(0)

    @pl.when(even == 1)
    def _():
        up.wait_recv()

    @pl.when(even == 0)
    def _():
        down.wait_recv()

    rows_out(1)
    half(1)

    @pl.when((even == 1) & (y > 0))
    def _():
        up.start()

    @pl.when((even == 0) & (y < 3))
    def _():
        down.start()

    rows_out(2)
    rows_out(3)

    @pl.when((even == 1) & (y > 0))
    def _():
        down.wait_recv()

    @pl.when((even == 0) & (y < 3))
    def _():
        up.wait_recv()

    rows_out(4)

    @pl.when(y > 0)
    def _():
        up.wait_send()

    @pl.when(y < 3)
    def _():
        down.wait_send()

    for side in range(2):
        ec_copies[side].wait_send()
        for k in range(8):
            edges(side, k).wait_send()
    for p in range(2):
        for d in range(1, 8):
            forward(p, d).wait_send()
    for p in range(5):
        finish(p)


def local(tracers, courant, assignment, species_gain, w_in, b_in, w_mid, b_mid, w_out, b_out):
    f32, bf16 = jnp.float32, jnp.bfloat16
    dma = pltpu.SemaphoreType.DMA
    operands = (
        tracers, courant, assignment.reshape(1, 80), species_gain.reshape(1, 80), w_in.T, b_in.reshape(1, 256),
        w_mid, b_mid, w_out, b_out.reshape(1, 80),
    )
    scratch = [
        ((10, 8, 16, 128), f32), ((2, 80, 8, 128), f32), ((22, 80, 128), f32), ((2, 80, 128), f32), ((80, 128), f32), ((8, 80, 128), f32),
        ((5, 80, 8, 128), f32), ((2, 16, 128), f32), ((2, 8, 128), f32), ((8, 128), f32), ((8, 128), f32),
        ((8, 128), f32), ((128, 128), f32), ((2, 80, 128), f32), ((16, 8, 128), f32), ((17, 8, 128), f32),
        ((2, 2, 8, 128), f32),
        ((1, 80), jnp.int32), ((1, 80), f32), ((80, 256), bf16), ((1, 256), f32), ((2, 256, 256), bf16),
        ((2, 256), f32), ((80, 256), bf16), ((1, 80), f32),
        ((256, 80), bf16), ((80, 256), bf16), ((3, 256, 128), f32), ((80, 128), f32), ((80, 128), f32),
    ]
    semaphores = [
        dma((2, 8)), dma((2, 8)), dma((2,)), dma((10,)), dma((2, 8)), dma((2, 8)), pltpu.SemaphoreType.REGULAR((2,)),
        dma((2,)), dma((2,)), dma((2,)), dma((2,)), dma((2,)), dma((2,)), dma((5, 8)), dma((5, 8)), dma((5,)),
    ]
    return pl.pallas_call(
        kernel,
        out_shape=jax.ShapeDtypeStruct(tracers.shape, f32),
        in_specs=[pl.BlockSpec(memory_space=pl.ANY)] * len(operands),
        out_specs=pl.BlockSpec(memory_space=pl.ANY),
        scratch_shapes=[pltpu.VMEM(*s) for s in scratch] + semaphores,
        compiler_params=pltpu.CompilerParams(
            collective_id=0, has_side_effects=True, vmem_limit_bytes=VM
        ),
        cost_estimate=pl.CostEstimate(flops=704_000_000, bytes_accessed=4_000_000, transcendentals=1_600_000),
    )(*operands)


def solution(mesh):
    in_specs = (P("trc", None, "ty", "tx"), P(None, "trc", "ty", "tx")) + (P(),) * 8
    out_specs = P("trc", None, "ty", "tx")
    return jax.shard_map(local, mesh=mesh, in_specs=in_specs, out_specs=out_specs, check_vma=False)
```

```python
import functools

import jax
import jax.numpy as jnp
from jax import lax
from jax.experimental import pallas as pl
from jax.experimental.pallas import tpu as pltpu
from jax.sharding import PartitionSpec as P

MESH = pl.DeviceIdType.MESH
VM = 60 * 1024 * 1024
GROUPS = (2, 3, 2, 6, 3)
STARTS_EVEN = (11, 13, 9, 3, 0)
STARTS_ODD = (3, 0, 5, 7, 13)


def upwind(f):
    up, down = jnp.maximum(f, 0.0), jnp.minimum(f, 0.0)
    p2, m2 = 0.5 * up * up, 0.5 * down * down
    return up, p2, p2 * (1.0 - (2.0 / 3.0) * up), down, m2, m2 * (1.0 + (2.0 / 3.0) * down)


def edge(a, b, c, d):
    return (7.0 / 12.0) * (b + c) - (1.0 / 12.0) * (a + d)


def sweep_lanes(q, coef):
    p1, p2, p3, m1, m2, m3 = coef
    left = edge(pltpu.roll(q, 2, 1), pltpu.roll(q, 1, 1), q, pltpu.roll(q, 127, 1))
    right = pltpu.roll(left, 127, 1)
    slope = right - left
    curve = 6.0 * q - 3.0 * (left + right)
    out_right = p1 * right - p2 * slope + p3 * curve
    out_left = m1 * left - m2 * slope - m3 * curve
    return q - out_right + out_left + pltpu.roll(out_right, 1, 1) - pltpu.roll(out_left, 127, 1)


def gelu(v):
    inner = v * (0.7978845608028654 + (0.7978845608028654 * 0.044715) * (v * v))
    half = 0.5 * v
    return (half + half * jnp.tanh(inner)).astype(jnp.bfloat16)


def column_of(row, size):
    at = lax.broadcasted_iota(jnp.int32, (size, size), 0)
    to = lax.broadcasted_iota(jnp.int32, (size, size), 1)
    return jnp.sum(jnp.where(at == to, row, 0.0), axis=1, keepdims=True)


def kernel(
    x_ref, c_ref, as_ref, gain_ref, win_ref, bin_ref, wmid_ref, bmid_ref, wout_ref, bout_ref,
    o_ref, b_ref,
    xv, got, swept, strip, fixed, adv, back, cv, c1h, eco, ecl, ecr, q_out, q_in, cc, cf, sc,
    v_as, v_gain, v_win, v_bin, v_wmid, v_bmid, v_wout, v_bout,
    first_w, last_w, bias_b, last_b, gain_b,
    fs, fr, fl, lw, qs, qr, ready, es, er, c1s, c1r, hs, hr, os_, or_, ol, bl,
):
    me, y, x = lax.axis_index("trc"), lax.axis_index("ty"), lax.axis_index("tx")
    even = 1 - lax.rem(y, 2)
    left, right = {"tx": lax.rem(x + 15, 16)}, {"tx": lax.rem(x + 1, 16)}

    def remote(src, dst, send, recv, to):
        return pltpu.make_async_remote_copy(src, dst, send, recv, device_id=to, device_id_type=MESH)

    def peer(d):
        return lax.rem(me + d, 8)

    loads = [
        pltpu.make_async_copy(src, dst, lw.at[i])
        for i, (src, dst) in enumerate((
            (c_ref.at[:, 0], cv), (x_ref, xv), (as_ref, v_as), (gain_ref, v_gain), (win_ref, v_win), (bin_ref, v_bin),
            (wmid_ref, v_wmid), (bmid_ref, v_bmid), (wout_ref, v_wout), (bout_ref, v_bout),
        ))
    ]
    for load in loads:
        load.start()

    c1h[...] = jnp.zeros((2, 8, 128), jnp.float32)
    barrier = pltpu.get_barrier_semaphore()
    first = lax.rem(x, 2) == 0

    @pl.when(first)
    def _():
        for side in (left, right):
            for k in range(8):
                pl.semaphore_signal(barrier, inc=1, device_id={"trc": k, **side}, device_id_type=MESH)

    for d in range(1, 8):
        pl.semaphore_signal(barrier, inc=1, device_id={"trc": peer(d)}, device_id_type=MESH)
    for d in (1, 3):
        pl.semaphore_signal(barrier, inc=1, device_id={"ty": lax.rem(y + d, 4)}, device_id_type=MESH)

    lane8 = lax.broadcasted_iota(jnp.int32, (8, 128), 1)
    lane16 = lax.broadcasted_iota(jnp.int32, (16, 128), 1)
    row16 = lax.broadcasted_iota(jnp.int32, (16, 128), 0)

    loads[0].wait()
    c0 = cv[0]
    wind = jnp.zeros((16, 128), jnp.float32)
    for i in range(8):
        wind = jnp.where((lane16 // 16 == i) & (row16 % 8 == i), pltpu.roll(c0, (16 * i + 8) % 128, 1), wind)
    eco[...] = jnp.zeros((8, 128), jnp.float32)
    eco[0:1, :] = jnp.sum(wind[0:8], axis=0, keepdims=True)
    eco[1:2, :] = jnp.sum(wind[8:16], axis=0, keepdims=True)

    @pl.when(y == 0)
    def _():
        swept[0:3] = jnp.zeros((3, 80, 128), jnp.float32)

    @pl.when(y == 3)
    def _():
        swept[19:22] = jnp.zeros((3, 80, 128), jnp.float32)

    halves = (8 * even, 8 * (1 - even))

    def forward(p, d):
        k = peer(d)
        rows = pl.ds(pl.multiple_of(halves[p], 8), 8)
        return remote(
            x_ref.at[:, k, rows], got.at[p, pl.ds(10 * me, 10)], fs.at[p, k], fr.at[p, me], {"trc": k}
        )

    def arriving(p, d):
        k = peer(d)
        there = got.at[p, pl.ds(10 * k, 10)]
        return remote(there, there, fs.at[p, k], fr.at[p, k], {"trc": k})

    def own(p):
        rows = pl.ds(pl.multiple_of(halves[p], 8), 8)
        return pltpu.make_async_copy(x_ref.at[:, me, rows], got.at[p, pl.ds(10 * me, 10)], fl.at[p])

    loads[1].wait()
    xv2 = xv.reshape(1280, 128)
    at16 = lane8 % 16

    @pl.loop(0, 10, unroll=5)
    def _(g):
        part = [jnp.zeros((8, 128), jnp.float32)] * 2
        for h in range(2):
            for i in range(8):
                v = pltpu.roll(xv2[pl.ds(g * 128 + 8 * h + i, 8, stride=16), :], (16 * i + 8) % 128, 1)
                part[h] = jnp.where(lane8 // 16 == i, v, part[h])
        q = jnp.where(at16 < 8, pltpu.roll(part[1], 125, 1), pltpu.roll(part[1], 3, 1))
        q_out[pl.ds(g, 8, stride=16), :] = jnp.where((at16 >= 5) & (at16 <= 10), part[0], q)

    q_out3 = q_out.reshape(8, 16, 128)

    def edges(side, k):
        return remote(
            q_out3.at[k, pl.ds(0, 10)], q_in.at[1 - side, pl.ds(10 * me, 10)], qs.at[side, k], qr.at[1 - side, me],
            {"trc": k, **(left, right)[side]},
        )

    ec_copies = (remote(eco, ecr, es.at[0], er.at[0], left), remote(eco, ecl, es.at[1], er.at[1], right))

    def send_edges(side):
        ec_copies[side].start()
        for k in range(8):
            edges(side, k).start()

    def send_half(p):
        for d in range(1, 8):
            forward(p, d).start()
        own(p).start()

    def greeted(side):
        pl.semaphore_wait(ready.at[side], 8)

    @pl.when(first)
    def _():
        pl.semaphore_wait(barrier, 9)
        send_half(0)
        greeted(1)
        send_edges(1)

        @pl.when(x > 0)
        def _():
            greeted(0)
            send_edges(0)

        send_half(1)

    @pl.when(jnp.logical_not(first))
    def _():
        pl.semaphore_wait(barrier, 25)
        for side, to in enumerate((left, right)):
            for k in range(8):
                pl.semaphore_signal(ready.at[1 - side], inc=1, device_id={"trc": k, **to}, device_id_type=MESH)
        send_edges(1)
        send_edges(0)
        send_half(0)
        send_half(1)

    wind_up = remote(cv.at[1, pl.ds(0, 1)], c1h.at[1, pl.ds(0, 1)], c1s.at[0], c1r.at[0], {"ty": y - 1})
    wind_down = remote(cv.at[1, pl.ds(15, 1)], c1h.at[0, pl.ds(0, 1)], c1s.at[1], c1r.at[1], {"ty": y + 1})

    @pl.when(y > 0)
    def _():
        wind_up.start()

    @pl.when(y < 3)
    def _():
        wind_down.start()

    for load in loads[2:]:
        load.wait()
    species = lax.broadcasted_iota(jnp.int32, (80, 80), 1)
    held = column_of(v_as[...].astype(jnp.float32), 80).astype(jnp.int32)
    chosen = held == species
    pick = jnp.where(chosen, 1.0, 0.0).astype(jnp.bfloat16)
    first_w[...] = lax.dot_general(
        v_win[...], pick, (((0,), (1,)), ((), ())), preferred_element_type=jnp.float32
    ).astype(jnp.bfloat16)
    last_w[...] = jnp.dot(pick, v_wout[...], preferred_element_type=jnp.float32).astype(jnp.bfloat16)
    gain_b[...] = jnp.broadcast_to(jnp.sum(jnp.where(chosen, v_gain[...], 0.0), axis=1, keepdims=True), (80, 128))
    last_b[...] = jnp.broadcast_to(jnp.sum(jnp.where(chosen, v_bout[...], 0.0), axis=1, keepdims=True), (80, 128))
    own_bias = pltpu.make_async_copy(last_b.at[pl.ds(10 * me, 10)], b_ref, bl)
    own_bias.start()
    bias_b[0] = jnp.broadcast_to(column_of(v_bin[...], 256), (256, 128))
    bias_b[1] = jnp.broadcast_to(column_of(v_bmid[0:1, :], 256), (256, 128))
    bias_b[2] = jnp.broadcast_to(column_of(v_bmid[1:2, :], 256), (256, 128))

    at_left = 0.5 * (pltpu.roll(c0, 1, 1) + c0)
    at_right = pltpu.roll(at_left, 127, 1)
    coef = upwind(at_right)[:3] + upwind(at_left)[3:]
    for i in range(6):
        cc[:, i, :] = coef[i]

    @pl.when(x == 0)
    def _():
        greeted(0)
        send_edges(0)

    inner = lane8 % 16 < 8

    def strip_coefficients():
        for copy in ec_copies:
            copy.wait_recv()
        for side in range(2):
            for k in range(8):
                there = q_in.at[side, pl.ds(10 * k, 10)]
                remote(there, there, qs.at[side, k], qr.at[side, k], {"trc": k, **(left, right)[side]}).wait_recv()
        winds = (jnp.where(inner, ecl[...], eco[...]), jnp.where(inner, eco[...], ecr[...]))
        for side, wind8 in enumerate(winds):
            at_left = 0.5 * (pltpu.roll(wind8, 1, 1) + wind8)
            at_right = pltpu.roll(at_left, 127, 1)
            coef = upwind(at_right)[:3] + upwind(at_left)[3:]
            for i in range(6):
                sc[side, 0, i : i + 1, :] = coef[i][0:1]
                sc[side, 1, i : i + 1, :] = coef[i][1:2]

    @pl.when(y > 0)
    def _():
        wind_up.wait_send()
        wind_down.wait_recv()

    @pl.when(y < 3)
    def _():
        wind_down.wait_send()
        wind_up.wait_recv()

    c1 = cv[1]
    above = jnp.where(row16 == 0, c1h[0, 0:1, :], pltpu.roll(c1, 1, 0))
    coef = upwind(0.5 * (above + c1))
    for i in range(6):
        cf[0:16, i, :] = coef[i]
    coef = upwind(0.5 * (c1[15:16] + c1h[1, 0:1, :]))
    for i in range(6):
        cf[16, i : i + 1, :] = coef[i]

    got2 = [got.at[p].reshape(640, 128) for p in range(2)]
    back2 = [back.at[p].reshape(640, 128) for p in range(5)]

    def row_coef(ref, *at):
        return [ref[(*at, pl.ds(i, 1), slice(None))] for i in range(6)]

    def half(p):
        base = halves[p]
        for d in range(1, 8):
            arriving(p, d).wait_recv()
        own(p).wait()

        @pl.loop(0, 10, unroll=5)
        def _(g):
            e = jnp.zeros((8, 128), jnp.float32)
            for i in range(8):
                q = got2[p][pl.ds(g * 64 + i, 8, stride=8), :]
                e = jnp.where(lane8 // 16 == i, pltpu.roll(q, (16 * i + 8) % 128, 1), e)
            strip[p, pl.ds(pl.multiple_of(g * 8, 8), 8), :] = e

        @pl.loop(0, 8, unroll=2)
        def _(i):
            coef = row_coef(cc, base + i)
            for g in range(0, 80, 16):
                q = got2[p][pl.ds(g * 8 + i, 16, stride=8), :]
                swept[base + i + 3, g : g + 16, :] = sweep_lanes(q, coef)

        if p == 0:
            strip_coefficients()
        coefs = [row_coef(sc, side, base // 8) for side in range(2)]
        h = base // 8
        for g in range(10):
            mine = strip[p, 8 * g : 8 * g + 8, :]
            before = pltpu.roll(q_in[0, 8 * g : 8 * g + 8, :], 3 * h, 1)
            after = pltpu.roll(q_in[1, 8 * g : 8 * g + 8, :], lax.rem(128 - 3 * h, 128), 1)
            new_left = sweep_lanes(jnp.where(inner, before, mine), coefs[0])
            new_right = sweep_lanes(jnp.where(inner, mine, after), coefs[1])
            fixed[8 * g : 8 * g + 8, :] = jnp.where(inner, new_right, new_left)
        sides = (lane8 < 3) | (lane8 >= 125)
        for i in range(8):
            for g in range(0, 80, 8):
                at = (base + i + 3, pl.ds(g, 8), slice(None))
                swept[at] = jnp.where(sides, pltpu.roll(fixed[g : g + 8, :], 120 - 16 * i, 1), swept[at])

    def rows_out(p):
        n = GROUPS[p]
        start = STARTS_ODD[p] + even * (STARTS_EVEN[p] - STARTS_ODD[p])

        @pl.loop(0, 10, unroll=2)
        def _(g):
            at = pl.ds(pl.multiple_of(g * 8, 8), 8)
            s = [swept[start + t, at, :] for t in range(n + 6)]
            e = [edge(*s[j : j + 4]) for j in range(n + 3)]
            flux = [None] * (n + 1)
            for j in range(n + 2):
                slope = e[j + 1] - e[j]
                curve = 6.0 * s[j + 2] - 3.0 * (e[j] + e[j + 1])
                if j <= n:
                    p1, p2, p3 = (cf[start + j, i : i + 1, :] for i in range(3))
                    flux[j] = p1 * e[j + 1] - p2 * slope + p3 * curve
                if j >= 1:
                    m1, m2, m3 = (cf[start + j - 1, i : i + 1, :] for i in range(3, 6))
                    flux[j - 1] = flux[j - 1] + (m1 * e[j] - m2 * slope - m3 * curve)
            for t in range(n):
                adv[t, at, :] = s[t + 3] - (flux[t + 1] - flux[t])

        wide = lambda v: jnp.concatenate([v] * n, axis=1)
        h = jnp.concatenate([(adv[t] * gain_b[...]).astype(jnp.bfloat16) for t in range(n)], axis=1)
        h = gelu(jnp.dot(first_w[...], h, preferred_element_type=jnp.float32) + wide(bias_b[0]))
        for m in range(2):
            h = gelu(jnp.dot(v_wmid[m], h, preferred_element_type=jnp.float32) + wide(bias_b[m + 1]))
        tend = jnp.dot(last_w[...], h, preferred_element_type=jnp.float32)
        for t in range(n):
            back2[p][pl.ds(t, 80, stride=8), :] = adv[t] + tend[:, 128 * t : 128 * t + 128]
        rows = pl.ds(start, n)
        for d in range(1, 8):
            k = peer(d)
            remote(
                back.at[p, pl.ds(10 * k, 10), pl.ds(0, n)], o_ref.at[:, me, rows], os_.at[p, k], or_.at[p, me], {"trc": k}
            ).start()
        pltpu.make_async_copy(back.at[p, pl.ds(10 * me, 10), pl.ds(0, n)], o_ref.at[:, me, rows], ol.at[p]).start()

    def finish(p):
        n = GROUPS[p]
        rows = pl.ds(STARTS_ODD[p] + even * (STARTS_EVEN[p] - STARTS_ODD[p]), n)
        for d in range(1, 8):
            k = peer(d)
            remote(
                back.at[p, pl.ds(10 * k, 10), pl.ds(0, n)], o_ref.at[:, k, rows], os_.at[p, k], or_.at[p, k], {"trc": k}
            ).wait()
        pltpu.make_async_copy(back.at[p, pl.ds(10 * me, 10), pl.ds(0, n)], o_ref.at[:, me, rows], ol.at[p]).wait()

    down = remote(swept.at[pl.ds(16, 3)], swept.at[pl.ds(0, 3)], hs.at[0], hr.at[0], {"ty": y + 1})
    up = remote(swept.at[pl.ds(3, 3)], swept.at[pl.ds(19, 3)], hs.at[1], hr.at[1], {"ty": y - 1})

    half(0)

    @pl.when(even == 1)
    def _():
        down.start()

    @pl.when(even == 0)
    def _():
        up.start()

    rows_out(0)

    @pl.when(even == 1)
    def _():
        up.wait_recv()

    @pl.when(even == 0)
    def _():
        down.wait_recv()

    rows_out(1)
    half(1)

    @pl.when((even == 1) & (y > 0))
    def _():
        up.start()

    @pl.when((even == 0) & (y < 3))
    def _():
        down.start()

    rows_out(2)
    rows_out(3)

    @pl.when((even == 1) & (y > 0))
    def _():
        down.wait_recv()

    @pl.when((even == 0) & (y < 3))
    def _():
        up.wait_recv()

    rows_out(4)

    @pl.when(y > 0)
    def _():
        up.wait_send()

    @pl.when(y < 3)
    def _():
        down.wait_send()

    for side in range(2):
        ec_copies[side].wait_send()
        for k in range(8):
            edges(side, k).wait_send()
    for p in range(2):
        for d in range(1, 8):
            forward(p, d).wait_send()
    own_bias.wait()
    for p in range(5):
        finish(p)


def local(tracers, courant, assignment, species_gain, w_in, b_in, w_mid, b_mid, w_out, b_out):
    f32, bf16 = jnp.float32, jnp.bfloat16
    dma = pltpu.SemaphoreType.DMA
    operands = (
        tracers, courant, assignment.reshape(1, 80), species_gain.reshape(1, 80), w_in.T, b_in.reshape(1, 256),
        w_mid, b_mid, w_out, b_out.reshape(1, 80),
    )
    scratch = [
        ((10, 8, 16, 128), f32), ((2, 80, 8, 128), f32), ((22, 80, 128), f32), ((2, 80, 128), f32), ((80, 128), f32), ((8, 80, 128), f32),
        ((5, 80, 8, 128), f32), ((2, 16, 128), f32), ((2, 8, 128), f32), ((8, 128), f32), ((8, 128), f32),
        ((8, 128), f32), ((128, 128), f32), ((2, 80, 128), f32), ((16, 8, 128), f32), ((17, 8, 128), f32),
        ((2, 2, 8, 128), f32),
        ((1, 80), jnp.int32), ((1, 80), f32), ((80, 256), bf16), ((1, 256), f32), ((2, 256, 256), bf16),
        ((2, 256), f32), ((80, 256), bf16), ((1, 80), f32),
        ((256, 80), bf16), ((80, 256), bf16), ((3, 256, 128), f32), ((80, 128), f32), ((80, 128), f32),
    ]
    semaphores = [
        dma((2, 8)), dma((2, 8)), dma((2,)), dma((10,)), dma((2, 8)), dma((2, 8)), pltpu.SemaphoreType.REGULAR((2,)),
        dma((2,)), dma((2,)), dma((2,)), dma((2,)), dma((2,)), dma((2,)), dma((5, 8)), dma((5, 8)), dma((5,)), pltpu.SemaphoreType.DMA,
    ]
    result, bias = pl.pallas_call(
        kernel,
        out_shape=(jax.ShapeDtypeStruct(tracers.shape, f32), jax.ShapeDtypeStruct((10, 128), f32)),
        in_specs=[pl.BlockSpec(memory_space=pl.ANY)] * len(operands),
        out_specs=[pl.BlockSpec(memory_space=pl.ANY)] * 2,
        scratch_shapes=[pltpu.VMEM(*s) for s in scratch] + semaphores,
        compiler_params=pltpu.CompilerParams(
            collective_id=0, has_side_effects=True, vmem_limit_bytes=VM
        ),
        cost_estimate=pl.CostEstimate(flops=704_000_000, bytes_accessed=4_000_000, transcendentals=1_600_000),
    )(*operands)
    return result + bias[:, None, None, :]


def solution(mesh):
    in_specs = (P("trc", None, "ty", "tx"), P(None, "trc", "ty", "tx")) + (P(),) * 8
    out_specs = P("trc", None, "ty", "tx")
    return jax.shard_map(local, mesh=mesh, in_specs=in_specs, out_specs=out_specs, check_vma=False)
```
